512 devices in a mesh: vtx: 64 (over z, y), pose: 8 (over x, core).
Axes of the slice: x: 4, y: 8, z: 8, core: 2. Of those that a mesh axis runs over, the one named last changes fastest.
Arguments:
- skin_weights: bfloat16 [524288, 128], P('vtx'), may hold values from -1.1 to 1.1
- bone_ids: int32 [2048, 4], P('vtx'), may hold values from 0 to 127, as said below
- slot_mask: int32 [2048, 4], P('vtx'), may hold values 0 or 1
- pose_coeffs: bfloat16 [128, 32, 2048], P(None, None, 'pose'), may hold values from -9 to 9
Outputs:
- projected: bfloat16 [524288, 2048], P('vtx', 'pose')
The draws below stay inside these ranges and needn't reach their ends.
Inputs may be any that keep to these rules, and one draw needn't show every extreme that they name: `bone_ids`: the 4 bone ids of a block are distinct.
All inputs are finite; a program needn't handle non-finite values. No bound on the sum of `slot_mask` on one device may be relied on, other than what follows from the above.
Results may differ from the reference program's by a relative error of at most 0.012.
Values may be sent and summed in bfloat16 or wider, within the bound.
A program may use at most 64 MiB of HBM per device.

```python
import math
import jax
import jax.numpy as jnp
from jax import lax

POSE_DEV = 256
BLOCK_ROWS = 256
SLOTS = 4
SHAPES = 32
BONES = 128
WINDOW = 16
RANK = 64
SWEEPS = 3
ROWS = 524288
POSES = 2048
BLOCKS = 2048
N_POSE = 8


def draw_skin_weights(key, part):
    key = jax.random.fold_in(key, 11)
    base_key, scale_key = jax.random.split(key)
    place = jnp.arange(ROWS, dtype=jnp.float32)[:, None] / ROWS
    base_values = jnp.clip(jax.random.normal(base_key, (ROWS, SLOTS * SHAPES), jnp.float32), -4.0, 4.0)
    row_scale = jnp.exp(jax.random.uniform(scale_key, (ROWS, 1), jnp.float32, math.log(0.5), math.log(1.5)))
    rising = jnp.exp(place * math.log(4.0))
    return (base_values * row_scale * rising / 24.0).astype(jnp.bfloat16)


def draw_bone_ids(key, part):
    key = jax.random.fold_in(key, 23)
    scores = jax.random.randint(key, (BLOCKS, WINDOW), 0, 1048576) * WINDOW + jnp.arange(WINDOW, dtype=jnp.int32)[None, :]
    offsets = jnp.argsort(scores, axis=1, stable=True)[:, :SLOTS].astype(jnp.int32)
    centers = jnp.arange(BLOCKS, dtype=jnp.int32) * BONES // BLOCKS
    return ((centers[:, None] + offsets - WINDOW // 2) % BONES).astype(jnp.int32)


def draw_pose_coeffs(key, part):
    key = jax.random.fold_in(key, 37)
    base_key, feature_key, pose_key = jax.random.split(key, 3)
    base_values = jnp.clip(jax.random.normal(base_key, (BONES, SHAPES, POSES), jnp.float32), -4.0, 4.0)
    feature_scale = jnp.exp(jax.random.uniform(feature_key, (BONES, SHAPES, 1), jnp.float32, math.log(0.5), math.log(1.5)))
    pose_scale = jnp.exp(jax.random.uniform(pose_key, (1, 1, POSES), jnp.float32, math.log(0.5), math.log(1.5)))
    return (base_values * feature_scale * pose_scale).astype(jnp.bfloat16)


def place_ends(values, stream_key, low, top_value):
    longest = values.shape.index(max(values.shape))
    spots = []
    for shift in (0, 1):
        where = [jax.random.randint(jax.random.fold_in(stream_key, axis), (), 0, length) for axis, length in enumerate(values.shape)]
        where[longest] = (where[longest] + shift) % values.shape[longest]
        spots.append(tuple(where))
    return values.at[spots[0]].set(low).at[spots[1]].set(top_value)


def setup_inputs(seed: int = 0) -> dict:
    seeds = jax.random.split(jax.random.key(seed), 5)
    return {
        "skin_weights": draw_skin_weights(jax.random.fold_in(seeds[4], 71), 0),
        "bone_ids": draw_bone_ids(jax.random.fold_in(seeds[4], 71), 0),
        "slot_mask": place_ends((jax.random.randint(seeds[2], (BLOCKS, SLOTS), 0, 4) < 3).astype(jnp.int32), jax.random.fold_in(seeds[2], 1), 0, 1),
        "pose_coeffs": draw_pose_coeffs(jax.random.fold_in(seeds[4], 71), 0),
    }


def orthonormal(columns):
    cross_gram = jnp.dot(columns.T.astype(jnp.float32), columns.astype(jnp.float32), precision=lax.Precision.HIGHEST, preferred_element_type=jnp.float32)
    lower_factor = jnp.linalg.cholesky(cross_gram)
    return jax.scipy.linalg.solve_triangular(lower_factor, columns.T, lower=True).T

def top_space(gram_matrix):
    columns = orthonormal(gram_matrix[:, :RANK])
    for sweep_index in range(SWEEPS - 1):
        columns = orthonormal(jnp.dot(gram_matrix.astype(jnp.float32), columns.astype(jnp.float32), precision=lax.Precision.HIGHEST, preferred_element_type=jnp.float32))
    return columns

def build_slab(skin_weights, bone_ids, slot_mask, coeffs):
    chosen = jnp.take(coeffs, bone_ids, axis=0) * slot_mask[:, :, None, None].astype(jnp.bfloat16)
    chosen = chosen.reshape(BLOCKS, SLOTS * SHAPES, -1).astype(jnp.float32)
    row_blocks = skin_weights.reshape(BLOCKS, BLOCK_ROWS, SLOTS * SHAPES).astype(jnp.float32)
    product = jnp.einsum('brk,bkp->brp', row_blocks, chosen)
    return product.reshape(ROWS, -1).astype(jnp.bfloat16)

def merge_pair(couple):
    joined = jnp.concatenate([couple[0], couple[1]], axis=1)
    gram_matrix = jnp.dot(joined.T.astype(jnp.float32), joined.astype(jnp.float32), precision=lax.Precision.HIGHEST, preferred_element_type=jnp.float32)
    return jnp.dot(joined.astype(jnp.float32), top_space(gram_matrix).astype(jnp.float32), precision=lax.Precision.HIGHEST, preferred_element_type=jnp.float32)

def reference(skin_weights, bone_ids, slot_mask, pose_coeffs):
    shards = pose_coeffs.reshape(BONES, SHAPES, N_POSE, POSE_DEV).transpose(2, 0, 1, 3)

    def leaf_sketch(coeffs):
        block_slab = build_slab(skin_weights, bone_ids, slot_mask, coeffs)
        gram_matrix = jnp.dot(block_slab.T.astype(jnp.float32), block_slab.astype(jnp.float32), preferred_element_type=jnp.float32)
        rotation = top_space(gram_matrix).astype(jnp.bfloat16)
        return jnp.dot(block_slab.astype(jnp.float32), rotation.astype(jnp.float32), preferred_element_type=jnp.float32)
    sketches = lax.map(leaf_sketch, shards)
    for level_index in range(N_POSE.bit_length() - 1):
        pairs = sketches.reshape(-1, 2, ROWS, RANK)
        sketches = lax.map(merge_pair, pairs)
    basis_rows = sketches[0].astype(jnp.bfloat16)
    cross_gram = jnp.dot(basis_rows.T.astype(jnp.float32), basis_rows.astype(jnp.float32), preferred_element_type=jnp.float32)
    lower_factor = jnp.linalg.cholesky(cross_gram)

    def project(coeffs):
        block_slab = build_slab(skin_weights, bone_ids, slot_mask, coeffs)
        moments = jnp.dot(basis_rows.T.astype(jnp.float32), block_slab.astype(jnp.float32), preferred_element_type=jnp.float32)
        coefficients = jax.scipy.linalg.cho_solve((lower_factor, True), moments).astype(jnp.bfloat16)
        return jnp.dot(basis_rows.astype(jnp.float32), coefficients.astype(jnp.float32), preferred_element_type=jnp.float32).astype(jnp.bfloat16)
    projected = lax.map(project, shards)
    return projected.transpose(1, 0, 2).reshape(ROWS, POSES)
```

```python
import functools

import jax
import jax.numpy as jnp
from jax import lax
from jax.experimental import pallas as pl
from jax.experimental.pallas import tpu as pltpu
from jax.sharding import PartitionSpec as P

RANK = 64
SWEEPS = 3
SHAPES = 32
SIDE = 8
F32 = jnp.float32
BF16 = jnp.bfloat16
HIGHEST = lax.Precision.HIGHEST
MESH = pl.DeviceIdType.MESH
VMEM = pl.BlockSpec(memory_space=pltpu.VMEM)
SMEM = pl.BlockSpec(memory_space=pltpu.SMEM)


def dot(a, b, dims, precision=None):
    return lax.dot_general(a, b, (dims, ((), ())), precision=precision, preferred_element_type=F32)


NN = ((1,), (0,))
NT = ((1,), (1,))
TN = ((0,), (0,))


def leaf_kernel(skin_ref, ids_ref, mask_ref, coeffs_ref, gram_ref, image_ref, chosen_ref, sums_ref):
    block_count, slots = ids_ref.shape
    block_rows = skin_ref.shape[0] // block_count
    sums_ref[...] = jnp.zeros_like(sums_ref)
    gram_ref[...] = jnp.zeros_like(gram_ref)

    def step(block, carry):
        for slot in range(slots):
            place = pl.multiple_of(ids_ref[block, slot] * SHAPES, SHAPES)
            values = coeffs_ref[pl.ds(place, SHAPES), :]
            active = mask_ref[block, slot] != 0
            chosen_ref[slot * SHAPES : (slot + 1) * SHAPES, :] = jnp.where(
                active, values, jnp.zeros_like(values)
            )
        rows = skin_ref[pl.ds(pl.multiple_of(block * block_rows, block_rows), block_rows), :]
        slab = dot(rows, chosen_ref[...], NN).astype(BF16)
        gram_ref[...] += dot(slab, slab, TN)
        image = dot(rows, slab, TN)
        for slot in range(slots):
            place = pl.multiple_of(ids_ref[block, slot] * SHAPES, SHAPES)
            active = mask_ref[block, slot] != 0
            values = image[slot * SHAPES : (slot + 1) * SHAPES, :]
            sums_ref[pl.ds(place, SHAPES), :] += jnp.where(active, values, jnp.zeros_like(values))
        return carry

    lax.fori_loop(0, block_count, step, 0)
    image_ref[...] = sums_ref[...].astype(BF16)


def my_place():
    vtx, pose = lax.axis_index("vtx"), lax.axis_index("pose")
    return vtx // SIDE, lax.rem(vtx, SIDE), pose


def vtx_peer(axis, z, y, pose, offset):
    if axis == "y":
        other = lax.rem(y + offset, SIDE)
        return other, (z * SIDE + other, pose)
    other = lax.rem(z + offset, SIDE)
    return other, (other * SIDE + y, pose)


def greet(devices):
    barrier = pltpu.get_barrier_semaphore()
    for device in devices:
        pl.semaphore_signal(barrier, inc=1, device_id=device, device_id_type=MESH)
    pl.semaphore_wait(barrier, len(devices))


def vtx_devices(z, y, pose):
    found = []
    for axis in ("y", "z"):
        for offset in range(1, SIDE):
            found.append(vtx_peer(axis, z, y, pose, offset)[1])
    return found


def exchange(parts, axis_of_half, source_of, target_of, send_sem, recv_sem, place):
    z, y, pose = place
    copies = []
    for half in range(parts):
        axis = axis_of_half[half]
        me = y if axis == "y" else z
        for offset in range(1, SIDE):
            other, device = vtx_peer(axis, z, y, pose, offset)
            copy = pltpu.make_async_remote_copy(
                src_ref=source_of(half, other),
                dst_ref=target_of(half, me),
                send_sem=send_sem.at[half, offset],
                recv_sem=recv_sem.at[half, me],
                device_id=device,
                device_id_type=MESH,
            )
            copy.start()
            copies.append(copy)
    return copies


def arrived(half, axis, target_of, send_sem, recv_sem, place):
    z, y, pose = place
    for offset in range(1, SIDE):
        other, device = vtx_peer(axis, z, y, pose, offset)
        pltpu.make_async_remote_copy(
            src_ref=target_of(half, other),
            dst_ref=target_of(half, other),
            send_sem=send_sem.at[half, offset],
            recv_sem=recv_sem.at[half, other],
            device_id=device,
            device_id_type=MESH,
        ).wait_recv()


def vtx_sum(source, first, second, total, sems, place):
    z, y, pose = place
    outer, inner = ("y", "z"), ("z", "y")
    mine = {"y": y, "z": z}
    sent = exchange(
        2, outer, lambda h, o: source.at[h, o], lambda h, m: first.at[h, m], sems[0], sems[1], place
    )
    for half in range(2):
        arrived(half, outer[half], lambda h, o: first.at[h, o], sems[0], sems[1], place)
        me = mine[outer[half]]
        first[half, me] = source[half, me]
        value = first[half, 0]
        for index in range(1, SIDE):
            value += first[half, index]
        second[half, mine[inner[half]]] = value
        sent += exchange_one(half, inner[half], second, sems[2], sems[3], place)
    for half in range(2):
        arrived(half, inner[half], lambda h, o: second.at[h, o], sems[2], sems[3], place)
        value = second[half, 0]
        for index in range(1, SIDE):
            value += second[half, index]
        total[half, mine[outer[half]]] = value
        sent += exchange_one(half, outer[half], total, sems[4], sems[5], place)
    for half in range(2):
        arrived(half, outer[half], lambda h, o: total.at[h, o], sems[4], sems[5], place)
    for copy in sent:
        copy.wait_send()


def exchange_one(half, axis, buffer, send_sem, recv_sem, place):
    z, y, pose = place
    me = y if axis == "y" else z
    copies = []
    for offset in range(1, SIDE):
        other, device = vtx_peer(axis, z, y, pose, offset)
        copy = pltpu.make_async_remote_copy(
            src_ref=buffer.at[half, me],
            dst_ref=buffer.at[half, me],
            send_sem=send_sem.at[half, offset],
            recv_sem=recv_sem.at[half, me],
            device_id=device,
            device_id_type=MESH,
        )
        copy.start()
        copies.append(copy)
    return copies


def to_chunks(matrix_ref, chunks_ref):
    depth = chunks_ref.shape[2]
    for half in range(2):
        for chunk in range(SIDE):
            chunks_ref[half, chunk] = matrix_ref[
                chunk * depth : (chunk + 1) * depth, half * 128 : (half + 1) * 128
            ]


def from_chunks(chunks_ref, matrix_ref):
    depth = chunks_ref.shape[2]
    for half in range(2):
        for chunk in range(SIDE):
            matrix_ref[chunk * depth : (chunk + 1) * depth, half * 128 : (half + 1) * 128] = chunks_ref[
                half, chunk
            ]


def gram_sum_kernel(part_ref, gram_ref, source, first, second, total, *sems):
    place = my_place()
    to_chunks(part_ref, source)
    greet(vtx_devices(*place))
    vtx_sum(source, first, second, total, sems, place)
    from_chunks(total, gram_ref)


def sum_scratch(rows):
    return [pltpu.VMEM((2, SIDE, rows // SIDE, 128), F32)] * 4 + [
        pltpu.SemaphoreType.DMA((2, SIDE))
    ] * 6


def inverse_factors(grams, identity_part):
    count = len(grams)
    groups = RANK // 8
    rows = [[gram[8 * g : 8 * g + 8] for g in range(groups)] for gram in grams]
    sublane = lax.broadcasted_iota(jnp.int32, (8, 128), 0)
    for n in range(count):
        for g in range(groups):
            rows[n][g] = rows[n][g] + identity_part[8 * g : 8 * g + 8]
    for p in range(groups):
        for n in range(count):
            own = rows[n]
            spread = [
                [
                    jnp.broadcast_to(own[g][:, RANK + 8 * p + c : RANK + 8 * p + c + 1], (8, 128))
                    for g in range(p, groups)
                ]
                for c in range(8)
            ]
            pivots = jnp.ones((8, 128), F32)
            for c in range(8):
                pivot = jnp.broadcast_to(spread[c][0][c : c + 1, :], (8, 128))
                pivots = jnp.where(sublane == c, pivot, pivots)
                inverse = 1.0 / pivot
                lead = jnp.broadcast_to(own[p][c : c + 1, :], (8, 128)) * inverse
                leads = [
                    jnp.broadcast_to(spread[d][0][c : c + 1, :], (8, 128)) * inverse
                    for d in range(c + 1, 8)
                ]
                for g in range(p, groups):
                    column = spread[c][g - p]
                    if g == p:
                        column = jnp.where(sublane > c, column, 0.0)
                    own[g] = own[g] - column * lead
                    for d in range(c + 1, 8):
                        spread[d][g - p] = spread[d][g - p] - column * leads[d - c - 1]
            own[p] = own[p] * lax.rsqrt(pivots)
    return [jnp.concatenate(own, axis=0)[:, :RANK] for own in rows]


def identity_lanes():
    row = lax.broadcasted_iota(jnp.int32, (RANK, 128), 0)
    lane = lax.broadcasted_iota(jnp.int32, (RANK, 128), 1)
    return jnp.where(row == lane, 1.0, 0.0).astype(F32)


def orthonormal(columns, identity_part):
    grams = []
    for value in columns:
        padded = jnp.concatenate([jnp.zeros_like(value), value], axis=0)
        grams.append(dot(value, padded, NT, HIGHEST))
    factors = inverse_factors(grams, identity_part)
    return [dot(factor, value, NN, HIGHEST) for factor, value in zip(factors, columns)]


def top_spaces(grams, identity_part):
    columns = orthonormal([gram[:RANK, :] for gram in grams], identity_part)
    for sweep in range(SWEEPS - 1):
        columns = orthonormal(
            [dot(value, gram, NN, HIGHEST) for value, gram in zip(columns, grams)], identity_part
        )
    return columns


def turn_kernel(gram_ref, coeffs_ref, turn_ref, sketch_ref):
    turn = top_spaces([gram_ref[...]], identity_lanes())[0].astype(BF16)
    turn_ref[...] = turn
    sketch_ref[...] = dot(turn, coeffs_ref[...], NT).astype(BF16)


def joint_kernel(sketch_ref, image_ref, turn_ref, all_ref, product_ref, gram_ref, *scratch):
    partial_ref, source, first, second, total = scratch[:5]
    sems = scratch[5:11]
    send_sem, recv_sem, gram_send, gram_recv = scratch[11:]
    place = my_place()
    z, y, pose = place
    vtx = z * SIDE + y
    poses = all_ref.shape[0]
    chips = poses // 2
    x, core = pose // 2, lax.rem(pose, 2)
    sibling = (vtx, x * 2 + 1 - core)
    pose_devices = [(vtx, lax.rem(pose + offset, poses)) for offset in range(1, poses)]
    greet(vtx_devices(*place) + pose_devices)

    def send(source_ref, slot, device, number):
        copy = pltpu.make_async_remote_copy(
            src_ref=source_ref,
            dst_ref=all_ref.at[slot],
            send_sem=send_sem.at[number],
            recv_sem=recv_sem.at[slot],
            device_id=device,
            device_id_type=MESH,
        )
        copy.start()
        return copy

    def wait_for(slot, device):
        pltpu.make_async_remote_copy(
            src_ref=all_ref.at[slot],
            dst_ref=all_ref.at[slot],
            send_sem=send_sem.at[0],
            recv_sem=recv_sem.at[slot],
            device_id=device,
            device_id_type=MESH,
        ).wait_recv()

    sent = []
    for offset in (1, chips - 1, 2):
        other = lax.rem(x + offset, chips)
        sent.append(send(sketch_ref, pose, (vtx, other * 2 + core), offset))
    sent.append(send(sketch_ref, pose, sibling, 0))
    all_ref[pose] = sketch_ref[...]
    for offset in (1, chips - 1, 2):
        other = lax.rem(x + offset, chips)
        slot = other * 2 + core
        wait_for(slot, (vtx, slot))
        sent.append(send(all_ref.at[slot], slot, sibling, chips + offset))
    for offset in range(chips):
        slot = lax.rem(x + offset, chips) * 2 + 1 - core
        wait_for(slot, sibling)
    for index in range(poses):
        partial_ref[index * RANK : (index + 1) * RANK, :] = dot(all_ref[index], image_ref[...], NN)
    to_chunks(partial_ref, source)
    vtx_sum(source, first, second, total, sems, place)
    from_chunks(total, product_ref)
    gram_ref[pose] = dot(turn_ref[...].astype(F32), product_ref[...], NT, HIGHEST)
    for offset in range(1, poses):
        copy = pltpu.make_async_remote_copy(
            src_ref=gram_ref.at[pose],
            dst_ref=gram_ref.at[pose],
            send_sem=gram_send.at[offset],
            recv_sem=gram_recv.at[pose],
            device_id=(vtx, lax.rem(pose + offset, poses)),
            device_id_type=MESH,
        )
        copy.start()
        sent.append(copy)
    for offset in range(1, poses):
        other = lax.rem(pose + offset, poses)
        pltpu.make_async_remote_copy(
            src_ref=gram_ref.at[other],
            dst_ref=gram_ref.at[other],
            send_sem=gram_send.at[offset],
            recv_sem=gram_recv.at[other],
            device_id=(vtx, other),
            device_id_type=MESH,
        ).wait_recv()
    for copy in sent:
        copy.wait_send()


def block_diagonal(blocks):
    height, width = blocks[0].shape
    rows = []
    for index, block in enumerate(blocks):
        parts = []
        if index:
            parts.append(jnp.zeros((height, width * index), F32))
        parts.append(block)
        if index + 1 < len(blocks):
            parts.append(jnp.zeros((height, width * (len(blocks) - 1 - index)), F32))
        rows.append(jnp.concatenate(parts, axis=1) if len(parts) > 1 else parts[0])
    return jnp.concatenate(rows, axis=0) if len(rows) > 1 else rows[0]


def merge_kernel(gram_ref, product_ref, all_ref, basis_ref, coefficients_ref):
    identity_part = identity_lanes()
    width = 2 * RANK
    gram = gram_ref[...]
    merged = None
    while True:
        pairs = gram.shape[0] // width
        spaces = top_spaces(
            [gram[n * width : (n + 1) * width, n * width : (n + 1) * width] for n in range(pairs)],
            identity_part,
        )
        turn = block_diagonal(spaces)
        merged = turn if merged is None else dot(turn, merged, NN, HIGHEST)
        if pairs == 1:
            break
        gram = dot(dot(turn, gram, NN, HIGHEST), turn, NT, HIGHEST)
    merged = merged.astype(BF16)
    wide = merged.astype(F32)
    image = dot(wide, gram_ref[...], NN, HIGHEST)
    padded = jnp.concatenate([jnp.zeros_like(wide), wide], axis=0)
    factor = inverse_factors([dot(image, padded, NT, HIGHEST)], identity_part)[0]
    moments = dot(wide, product_ref[...], NN, HIGHEST)
    half_way = dot(factor, moments, NN, HIGHEST)
    coefficients_ref[...] = dot(factor, half_way, TN, HIGHEST).astype(BF16)
    basis_ref[...] = dot(merged, all_ref[...], NN).T.astype(BF16)


def project_kernel(ids_ref, mask_ref, skin_ref, basis_ref, coefficients_ref, out_ref, chosen_ref):
    slots = ids_ref.shape[1]
    blocks_here = out_ref.shape[0] // 256
    first = pl.program_id(0) * blocks_here
    for index in range(blocks_here):
        for slot in range(slots):
            place = pl.multiple_of(ids_ref[first + index, slot] * SHAPES, SHAPES)
            active = mask_ref[first + index, slot] != 0
            values = basis_ref[pl.ds(place, SHAPES), :]
            chosen_ref[index, slot * SHAPES : (slot + 1) * SHAPES, :] = jnp.where(
                active, values, jnp.zeros_like(values)
            )
        rows = skin_ref[index * 256 : (index + 1) * 256, :]
        basis = dot(rows, chosen_ref[index], NN).astype(BF16)
        out_ref[index * 256 : (index + 1) * 256, :] = dot(basis, coefficients_ref[...], NN).astype(BF16)


def params(**more):
    return pltpu.CompilerParams(vmem_limit_bytes=56 * 2**20, **more)


def per_device(skin_weights, bone_ids, slot_mask, pose_coeffs):
    rows, depth = skin_weights.shape
    bones, shapes, poses = pose_coeffs.shape
    coeffs = pose_coeffs.reshape(bones * shapes, poses)
    wide = bones * shapes
    shards = lax.axis_size("pose")
    joint = shards * RANK
    part, image = pl.pallas_call(
        leaf_kernel,
        out_shape=(
            jax.ShapeDtypeStruct((poses, poses), F32),
            jax.ShapeDtypeStruct((wide, poses), BF16),
        ),
        in_specs=[VMEM, SMEM, SMEM, VMEM],
        out_specs=(VMEM, VMEM),
        scratch_shapes=[pltpu.VMEM((depth, poses), BF16), pltpu.VMEM((wide, poses), F32)],
        compiler_params=params(),
        name="leaf",
    )(skin_weights, bone_ids, slot_mask, coeffs)
    gram = pl.pallas_call(
        gram_sum_kernel,
        out_shape=jax.ShapeDtypeStruct((poses, poses), F32),
        in_specs=[VMEM],
        out_specs=VMEM,
        scratch_shapes=sum_scratch(poses),
        compiler_params=params(collective_id=0, has_side_effects=True),
        name="gram_sum",
    )(part)
    turn, sketch = pl.pallas_call(
        turn_kernel,
        out_shape=(
            jax.ShapeDtypeStruct((RANK, poses), BF16),
            jax.ShapeDtypeStruct((RANK, wide), BF16),
        ),
        in_specs=[VMEM, VMEM],
        out_specs=(VMEM, VMEM),
        compiler_params=params(),
        name="turn",
    )(gram, coeffs)
    sketches, product, joint_gram = pl.pallas_call(
        joint_kernel,
        out_shape=(
            jax.ShapeDtypeStruct((shards, RANK, wide), BF16),
            jax.ShapeDtypeStruct((joint, poses), F32),
            jax.ShapeDtypeStruct((shards, RANK, joint), F32),
        ),
        in_specs=[VMEM, VMEM, VMEM],
        out_specs=(VMEM, VMEM, VMEM),
        scratch_shapes=[pltpu.VMEM((joint, poses), F32)]
        + sum_scratch(joint)
        + [
            pltpu.SemaphoreType.DMA((shards,)),
            pltpu.SemaphoreType.DMA((shards,)),
            pltpu.SemaphoreType.DMA((shards,)),
            pltpu.SemaphoreType.DMA((shards,)),
        ],
        compiler_params=params(collective_id=1, has_side_effects=True),
        name="joint",
    )(sketch, image, turn)
    basis, coefficients = pl.pallas_call(
        merge_kernel,
        out_shape=(
            jax.ShapeDtypeStruct((wide, RANK), BF16),
            jax.ShapeDtypeStruct((RANK, poses), BF16),
        ),
        in_specs=[VMEM, VMEM, VMEM],
        out_specs=(VMEM, VMEM),
        compiler_params=params(),
        name="merge",
    )(joint_gram.reshape(joint, joint), product, sketches.reshape(joint, wide))
    step_rows = 1024
    return pl.pallas_call(
        project_kernel,
        out_shape=jax.ShapeDtypeStruct((rows, poses), BF16),
        grid=(rows // step_rows,),
        in_specs=[
            SMEM,
            SMEM,
            pl.BlockSpec((step_rows, depth), lambda i: (i, 0)),
            VMEM,
            VMEM,
        ],
        out_specs=pl.BlockSpec((step_rows, poses), lambda i: (i, 0)),
        scratch_shapes=[pltpu.VMEM((step_rows // 256, depth, RANK), BF16)],
        compiler_params=params(),
        name="project",
    )(bone_ids, slot_mask, skin_weights, basis, coefficients)


def solution(mesh):
    in_specs = (P("vtx", None), P("vtx", None), P("vtx", None), P(None, None, "pose"))
    return jax.shard_map(
        per_device, mesh=mesh, in_specs=in_specs, out_specs=P("vtx", "pose"), check_vma=False
    )
```

```python
import functools

import jax
import jax.numpy as jnp
from jax import lax
from jax.experimental import pallas as pl
from jax.experimental.pallas import tpu as pltpu
from jax.sharding import PartitionSpec as P

RANK = 64
SWEEPS = 3
SHAPES = 32
SIDE = 8
F32 = jnp.float32
BF16 = jnp.bfloat16
HIGHEST = lax.Precision.HIGHEST
MESH = pl.DeviceIdType.MESH
VMEM = pl.BlockSpec(memory_space=pltpu.VMEM)
SMEM = pl.BlockSpec(memory_space=pltpu.SMEM)


def dot(a, b, dims, precision=None):
    return lax.dot_general(a, b, (dims, ((), ())), precision=precision, preferred_element_type=F32)


NN = ((1,), (0,))
NT = ((1,), (1,))
TN = ((0,), (0,))


def chosen_rows(ids_ref, mask_ref, source_ref, block):
    parts = []
    for slot in range(ids_ref.shape[0]):
        place = pl.multiple_of(ids_ref[slot, block] * SHAPES, SHAPES)
        values = source_ref[pl.ds(place, SHAPES), :]
        parts.append(jnp.where(mask_ref[slot, block] != 0, values, jnp.zeros_like(values)))
    return jnp.concatenate(parts, axis=0)


def leaf_kernel(skin_ref, ids_ref, mask_ref, coeffs_ref, gram_ref, image_ref, slab_ref, sums_ref):
    slots, block_count = ids_ref.shape
    block_rows = skin_ref.shape[0] // block_count
    group = slab_ref.shape[0] // block_rows
    sums_ref[...] = jnp.zeros_like(sums_ref)
    gram_ref[...] = jnp.zeros_like(gram_ref)

    def step(index, carry):
        images = []
        for inside in range(group):
            block = index * group + inside
            rows = skin_ref[pl.ds(pl.multiple_of(block * block_rows, block_rows), block_rows), :]
            slab = dot(rows, chosen_rows(ids_ref, mask_ref, coeffs_ref, block), NN).astype(BF16)
            slab_ref[inside * block_rows : (inside + 1) * block_rows, :] = slab
            images.append(dot(rows, slab, TN))
        gram_ref[...] += dot(slab_ref[...], slab_ref[...], TN)
        for inside in range(group):
            block = index * group + inside
            for slot in range(slots):
                place = pl.multiple_of(ids_ref[slot, block] * SHAPES, SHAPES)
                values = images[inside][slot * SHAPES : (slot + 1) * SHAPES, :]
                sums_ref[pl.ds(place, SHAPES), :] += jnp.where(
                    mask_ref[slot, block] != 0, values, jnp.zeros_like(values)
                )
        return carry

    lax.fori_loop(0, block_count // group, step, 0)
    image_ref[...] = sums_ref[...].astype(BF16)


def my_place():
    vtx, pose = lax.axis_index("vtx"), lax.axis_index("pose")
    return vtx // SIDE, lax.rem(vtx, SIDE), pose


def vtx_peer(axis, z, y, pose, offset):
    if axis == "y":
        other = lax.rem(y + offset, SIDE)
        return other, (z * SIDE + other, pose)
    other = lax.rem(z + offset, SIDE)
    return other, (other * SIDE + y, pose)


def greet(devices):
    barrier = pltpu.get_barrier_semaphore()
    for device in devices:
        pl.semaphore_signal(barrier, inc=1, device_id=device, device_id_type=MESH)
    pl.semaphore_wait(barrier, len(devices))


def vtx_devices(z, y, pose):
    found = []
    for axis in ("y", "z"):
        for offset in range(1, SIDE):
            found.append(vtx_peer(axis, z, y, pose, offset)[1])
    return found


def exchange(parts, axis_of_half, source_of, target_of, send_sem, recv_sem, place):
    z, y, pose = place
    copies = []
    for half in range(parts):
        axis = axis_of_half[half]
        me = y if axis == "y" else z
        for offset in range(1, SIDE):
            other, device = vtx_peer(axis, z, y, pose, offset)
            copy = pltpu.make_async_remote_copy(
                src_ref=source_of(half, other),
                dst_ref=target_of(half, me),
                send_sem=send_sem.at[half, offset],
                recv_sem=recv_sem.at[half, me],
                device_id=device,
                device_id_type=MESH,
            )
            copy.start()
            copies.append(copy)
    return copies


def arrived(half, axis, target_of, send_sem, recv_sem, place):
    z, y, pose = place
    for offset in range(1, SIDE):
        other, device = vtx_peer(axis, z, y, pose, offset)
        pltpu.make_async_remote_copy(
            src_ref=target_of(half, other),
            dst_ref=target_of(half, other),
            send_sem=send_sem.at[half, offset],
            recv_sem=recv_sem.at[half, other],
            device_id=device,
            device_id_type=MESH,
        ).wait_recv()


def vtx_sum(source, first, second, total, sems, place):
    z, y, pose = place
    outer, inner = ("y", "z"), ("z", "y")
    mine = {"y": y, "z": z}
    sent = exchange(
        2, outer, lambda h, o: source.at[h, o], lambda h, m: first.at[h, m], sems[0], sems[1], place
    )
    for half in range(2):
        arrived(half, outer[half], lambda h, o: first.at[h, o], sems[0], sems[1], place)
        me = mine[outer[half]]
        first[half, me] = source[half, me]
        value = first[half, 0]
        for index in range(1, SIDE):
            value += first[half, index]
        second[half, mine[inner[half]]] = value
        sent += exchange_one(half, inner[half], second, sems[2], sems[3], place)
    for half in range(2):
        arrived(half, inner[half], lambda h, o: second.at[h, o], sems[2], sems[3], place)
        value = second[half, 0]
        for index in range(1, SIDE):
            value += second[half, index]
        total[half, mine[outer[half]]] = value
        sent += exchange_one(half, outer[half], total, sems[4], sems[5], place)
    for half in range(2):
        arrived(half, outer[half], lambda h, o: total.at[h, o], sems[4], sems[5], place)
    for copy in sent:
        copy.wait_send()


def exchange_one(half, axis, buffer, send_sem, recv_sem, place):
    z, y, pose = place
    me = y if axis == "y" else z
    copies = []
    for offset in range(1, SIDE):
        other, device = vtx_peer(axis, z, y, pose, offset)
        copy = pltpu.make_async_remote_copy(
            src_ref=buffer.at[half, me],
            dst_ref=buffer.at[half, me],
            send_sem=send_sem.at[half, offset],
            recv_sem=recv_sem.at[half, me],
            device_id=device,
            device_id_type=MESH,
        )
        copy.start()
        copies.append(copy)
    return copies


def to_chunks(matrix_ref, chunks_ref):
    depth = chunks_ref.shape[2]
    for half in range(2):
        for chunk in range(SIDE):
            chunks_ref[half, chunk] = matrix_ref[
                chunk * depth : (chunk + 1) * depth, half * 128 : (half + 1) * 128
            ]


def from_chunks(chunks_ref, matrix_ref):
    depth = chunks_ref.shape[2]
    for half in range(2):
        for chunk in range(SIDE):
            matrix_ref[chunk * depth : (chunk + 1) * depth, half * 128 : (half + 1) * 128] = chunks_ref[
                half, chunk
            ]


def gram_sum_kernel(part_ref, gram_ref, source, first, second, total, *sems):
    place = my_place()
    to_chunks(part_ref, source)
    greet(vtx_devices(*place))
    vtx_sum(source, first, second, total, sems, place)
    from_chunks(total, gram_ref)


def sum_scratch(rows, groups=()):
    return [pltpu.VMEM((*groups, 2, SIDE, rows // SIDE, 128), F32)] * 4 + [
        pltpu.SemaphoreType.DMA((*groups, 2, SIDE))
    ] * 6


def inverse_factors(grams):
    count = len(grams)
    groups = RANK // 8
    sublane = lax.broadcasted_iota(jnp.int32, (8, 128), 0)
    lane = lax.broadcasted_iota(jnp.int32, (8, 128), 1)
    rows = [
        [gram[8 * g : 8 * g + 8] + jnp.where(lane == sublane + 8 * g, 1.0, 0.0) for g in range(groups)]
        for gram in grams
    ]
    squares = []
    for p in range(groups):
        for n in range(count):
            own = rows[n]
            spread = [
                [
                    jnp.broadcast_to(own[g][:, RANK + 8 * p + c : RANK + 8 * p + c + 1], (8, 128))
                    for g in range(p, groups)
                ]
                for c in range(8)
            ]
            pivots = jnp.ones((8, 128), F32)
            for c in range(8):
                pivot = jnp.broadcast_to(spread[c][0][c : c + 1, :], (8, 128))
                pivots = jnp.where(sublane == c, pivot, pivots)
                inverse = 1.0 / pivot
                lead = jnp.broadcast_to(own[p][c : c + 1, :], (8, 128)) * inverse
                leads = [
                    jnp.broadcast_to(spread[d][0][c : c + 1, :], (8, 128)) * inverse
                    for d in range(c + 1, 8)
                ]
                for g in range(p, groups):
                    column = spread[c][g - p]
                    if g == p:
                        column = jnp.where(sublane > c, column, 0.0)
                    own[g] = own[g] - column * lead
                    for d in range(c + 1, 8):
                        spread[d][g - p] = spread[d][g - p] - column * leads[d - c - 1]
            own[p] = own[p] * lax.rsqrt(pivots)
            squares.append((n, pivots))
    factors = [jnp.concatenate(own, axis=0)[:, :RANK] for own in rows]
    return factors, [[value for m, value in squares if m == n] for n in range(count)]


def factors_of(columns):
    grams = []
    for value in columns:
        padded = jnp.concatenate([jnp.zeros_like(value), value], axis=0)
        grams.append(dot(value, padded, NT, HIGHEST))
    return inverse_factors(grams)


def top_spaces(grams, out_ref):
    columns = []
    scaled = []
    for gram in grams:
        size = gram.shape[0]
        diagonal = lax.broadcasted_iota(jnp.int32, (size, size), 0) == lax.broadcasted_iota(
            jnp.int32, (size, size), 1
        )
        largest = jnp.max(
            jnp.max(jnp.where(diagonal, gram, 0.0), axis=0, keepdims=True), axis=1, keepdims=True
        )
        scaled.append(gram * (1.0 / largest))
        columns.append(scaled[-1][:RANK, :])
    for sweep in range(SWEEPS - 1):
        columns = [dot(value, gram, NN, HIGHEST) for value, gram in zip(columns, scaled)]
    factors, squares = factors_of(columns)
    worst = None
    for n, (factor, value) in enumerate(zip(factors, columns)):
        out_ref[n] = dot(factor, value, NN, HIGHEST)
        low = functools.reduce(jnp.minimum, squares[n])
        high = functools.reduce(jnp.maximum, squares[n])
        ratio = jnp.min(low) / jnp.max(high)
        good = ratio > 2e-5
        worst = good if worst is None else jnp.logical_and(worst, good)

    @pl.when(jnp.logical_not(worst))
    def _():
        row = lax.broadcasted_iota(jnp.int32, grams[0].shape, 0)
        lane = lax.broadcasted_iota(jnp.int32, grams[0].shape, 1)
        for n in range(len(grams)):
            out_ref[n] = jnp.where(row == lane, 1.0, 0.0).astype(F32)[:RANK]

        def sweep(index, carry):
            values = [dot(out_ref[n], gram, NN, HIGHEST) for n, gram in enumerate(grams)]
            for n, (factor, value) in enumerate(zip(factors_of(values)[0], values)):
                out_ref[n] = dot(factor, value, NN, HIGHEST)
            return carry

        lax.fori_loop(0, SWEEPS, sweep, 0)

    return [out_ref[n] for n in range(len(grams))]


def turn_kernel(gram_ref, coeffs_ref, turn_ref, sketch_ref, space_ref):
    turn = top_spaces([gram_ref[...]], space_ref)[0].astype(BF16)
    turn_ref[...] = turn
    sketch_ref[...] = dot(turn, coeffs_ref[...], NT).astype(BF16)


def joint_kernel(sketch_ref, image_ref, turn_ref, all_ref, product_ref, gram_ref, *scratch):
    source, first, second, total = scratch[:4]
    sems = scratch[4:10]
    send_sem, recv_sem, gram_send, gram_recv = scratch[10:]
    place = my_place()
    z, y, pose = place
    vtx = z * SIDE + y
    poses = all_ref.shape[0]
    chips = poses // 2
    width = 2 * RANK
    middle = RANK // 2
    x, core = pose // 2, lax.rem(pose, 2)
    sibling = (vtx, x * 2 + 1 - core)
    chip_at = [lax.rem(x + group, chips) for group in range(chips)]
    peer = [(vtx, chip * 2 + core) for chip in chip_at]
    outer, inner = ("y", "z"), ("z", "y")
    mine = {"y": y, "z": z}
    greet(vtx_devices(*place) + [(vtx, lax.rem(pose + offset, poses)) for offset in range(1, poses)])
    sent = []

    def send(source_ref, target_ref, arrival, device, number):
        copy = pltpu.make_async_remote_copy(
            src_ref=source_ref,
            dst_ref=target_ref,
            send_sem=send_sem.at[number],
            recv_sem=arrival,
            device_id=device,
            device_id_type=MESH,
        )
        copy.start()
        sent.append(copy)

    def wait_for(target_ref, arrival, device):
        pltpu.make_async_remote_copy(
            src_ref=target_ref,
            dst_ref=target_ref,
            send_sem=send_sem.at[0],
            recv_sem=arrival,
            device_id=device,
            device_id_type=MESH,
        ).wait_recv()

    def half_of(slot, half):
        return all_ref.at[slot, pl.ds(half * middle, middle)]

    def start_sum(group):
        for index in range(2):
            part = dot(all_ref[chip_at[group] * 2 + index], image_ref[...], NN)
            depth = width // SIDE
            for chunk in range(SIDE // 2):
                for half in range(2):
                    source[group, half, index * (SIDE // 2) + chunk] = part[
                        chunk * depth : (chunk + 1) * depth, half * 128 : (half + 1) * 128
                    ]
        sent.extend(
            exchange(
                2,
                outer,
                lambda h, o: source.at[group, h, o],
                lambda h, m: first.at[group, h, m],
                sems[0].at[group],
                sems[1].at[group],
                place,
            )
        )

    def second_leg(group):
        for half in range(2):
            arrived(
                half, outer[half], lambda h, o: first.at[group, h, o], sems[0].at[group], sems[1].at[group], place
            )
            me = mine[outer[half]]
            first[group, half, me] = source[group, half, me]
            value = first[group, half, 0]
            for index in range(1, SIDE):
                value += first[group, half, index]
            second[group, half, mine[inner[half]]] = value
            sent.extend(
                exchange_one(half, inner[half], second.at[group], sems[2].at[group], sems[3].at[group], place)
            )

    def third_leg(group):
        for half in range(2):
            arrived(
                half, inner[half], lambda h, o: second.at[group, h, o], sems[2].at[group], sems[3].at[group], place
            )
            value = second[group, half, 0]
            for index in range(1, SIDE):
                value += second[group, half, index]
            total[group, half, mine[outer[half]]] = value
            sent.extend(
                exchange_one(half, outer[half], total.at[group], sems[4].at[group], sems[5].at[group], place)
            )

    def end_sum(group):
        for half in range(2):
            arrived(
                half, outer[half], lambda h, o: total.at[group, h, o], sems[4].at[group], sems[5].at[group], place
            )
        row = pl.multiple_of(chip_at[group] * width, width)
        for half in range(2):
            product_ref[pl.ds(row, width), half * 128 : (half + 1) * 128] = total[group, half].reshape(width, 128)

    def gram_part(group):
        row = pl.multiple_of(chip_at[group] * width, width)
        gram_ref[chip_at[group], pose] = dot(
            turn_ref[...].astype(F32), product_ref[pl.ds(row, width), :], NT, HIGHEST
        )
        for offset in range(1, poses):
            copy = pltpu.make_async_remote_copy(
                src_ref=gram_ref.at[chip_at[group], pose],
                dst_ref=gram_ref.at[chip_at[group], pose],
                send_sem=gram_send.at[group, offset],
                recv_sem=gram_recv.at[group, pose],
                device_id=(vtx, lax.rem(pose + offset, poses)),
                device_id_type=MESH,
            )
            copy.start()
            sent.append(copy)

    def gram_arrived(group):
        for offset in range(1, poses):
            other = lax.rem(pose + offset, poses)
            chip = lax.rem(other // 2 + group, chips)
            wait_for(gram_ref.at[chip, other], gram_recv.at[group, other], (vtx, other))

    own = pose
    up, down, across = [chip_at[g] * 2 + core for g in (1, 3, 2)]
    send(sketch_ref, all_ref.at[own], recv_sem.at[0, own], peer[1], 0)
    send(sketch_ref, all_ref.at[own], recv_sem.at[0, own], peer[3], 1)
    send(sketch_ref, all_ref.at[own], recv_sem.at[0, own], sibling, 2)
    all_ref[own] = sketch_ref[...]
    other = sibling[1]
    wait_for(all_ref.at[other], recv_sem.at[0, other], sibling)
    start_sum(0)
    second_leg(0)
    wait_for(all_ref.at[down], recv_sem.at[0, down], peer[3])
    send(half_of(down, 0), half_of(down, 0), recv_sem.at[0, down], peer[1], 3)
    send(all_ref.at[down], all_ref.at[down], recv_sem.at[0, down], sibling, 4)
    wait_for(all_ref.at[up], recv_sem.at[0, up], peer[1])
    send(half_of(up, 1), half_of(up, 1), recv_sem.at[1, up], peer[3], 5)
    send(all_ref.at[up], all_ref.at[up], recv_sem.at[0, up], sibling, 6)
    third_leg(0)
    for group in (3, 1):
        slot = chip_at[group] * 2 + 1 - core
        wait_for(all_ref.at[slot], recv_sem.at[0, slot], sibling)
        start_sum(group)
    end_sum(0)
    gram_part(0)
    second_leg(3)
    second_leg(1)
    wait_for(half_of(across, 0), recv_sem.at[0, across], peer[3])
    send(half_of(across, 0), half_of(across, 0), recv_sem.at[0, across], sibling, 7)
    wait_for(half_of(across, 1), recv_sem.at[1, across], peer[1])
    send(half_of(across, 1), half_of(across, 1), recv_sem.at[1, across], sibling, 8)
    slot = chip_at[2] * 2 + 1 - core
    wait_for(half_of(slot, 0), recv_sem.at[0, slot], sibling)
    wait_for(half_of(slot, 1), recv_sem.at[1, slot], sibling)
    start_sum(2)
    third_leg(3)
    third_leg(1)
    second_leg(2)
    end_sum(1)
    gram_part(1)
    third_leg(2)
    end_sum(3)
    end_sum(2)
    gram_part(2)
    for group in (0, 1, 2):
        gram_arrived(group)
    for copy in sent:
        copy.wait_send()


def block_diagonal(blocks):
    height, width = blocks[0].shape
    rows = []
    for index, block in enumerate(blocks):
        parts = []
        if index:
            parts.append(jnp.zeros((height, width * index), F32))
        parts.append(block)
        if index + 1 < len(blocks):
            parts.append(jnp.zeros((height, width * (len(blocks) - 1 - index)), F32))
        rows.append(jnp.concatenate(parts, axis=1) if len(parts) > 1 else parts[0])
    return jnp.concatenate(rows, axis=0) if len(rows) > 1 else rows[0]


def merge_kernel(rows_ref, product_ref, all_ref, basis_ref, coefficients_ref, joint_ref, space_ref):
    width = 2 * RANK
    chips = rows_ref.shape[0]
    for chip in range(chips):
        for other in range(chips):
            behind = (chip - other) % chips == 1
            for index in range(2):
                if behind:
                    continue
                joint_ref[
                    chip * width + index * RANK : chip * width + (index + 1) * RANK,
                    other * width : (other + 1) * width,
                ] = rows_ref[other, 2 * chip + index]
    for chip in range(chips):
        other = (chip - 1) % chips
        joint_ref[chip * width : (chip + 1) * width, other * width : (other + 1) * width] = joint_ref[
            other * width : (other + 1) * width, chip * width : (chip + 1) * width
        ].T
    gram = joint_ref[...]
    merged = None
    while True:
        pairs = gram.shape[0] // width
        spaces = top_spaces(
            [gram[n * width : (n + 1) * width, n * width : (n + 1) * width] for n in range(pairs)],
            space_ref,
        )
        turn = block_diagonal(spaces)
        merged = turn if merged is None else dot(turn, merged, NN, HIGHEST)
        if pairs == 1:
            break
        gram = dot(dot(turn, gram, NN, HIGHEST), turn, NT, HIGHEST)
    merged = merged.astype(BF16)
    wide = merged.astype(F32)
    image = dot(wide, joint_ref[...], NN, HIGHEST)
    padded = jnp.concatenate([jnp.zeros_like(wide), wide], axis=0)
    factor = inverse_factors([dot(image, padded, NT, HIGHEST)])[0][0]
    moments = dot(wide, product_ref[...], NN, HIGHEST)
    half_way = dot(factor, moments, NN, HIGHEST)
    coefficients_ref[...] = dot(factor, half_way, TN, HIGHEST).astype(BF16)
    basis_ref[...] = dot(merged, all_ref[...], NN).T.astype(BF16)


def project_kernel(ids_ref, mask_ref, skin_ref, basis_ref, coefficients_ref, out_ref, rows_ref):
    block_count = ids_ref.shape[1]
    blocks_here = block_count // pl.num_programs(0)
    block_rows = out_ref.shape[0] // blocks_here
    first = pl.program_id(0) * blocks_here
    for index in range(blocks_here):
        chosen = chosen_rows(ids_ref, mask_ref, basis_ref, first + index)
        here = slice(index * block_rows, (index + 1) * block_rows)
        rows_ref[here, :] = dot(skin_ref[here, :], chosen, NN).astype(BF16)
    out_ref[...] = dot(rows_ref[...], coefficients_ref[...], NN).astype(BF16)


def params(mebibytes, **more):
    return pltpu.CompilerParams(vmem_limit_bytes=mebibytes * 2**20, **more)


def per_device(skin_weights, bone_ids, slot_mask, pose_coeffs):
    rows, depth = skin_weights.shape
    bones, shapes, poses = pose_coeffs.shape
    coeffs = pose_coeffs.reshape(bones * shapes, poses)
    wide = bones * shapes
    shards = lax.axis_size("pose")
    joint = shards * RANK
    bone_ids, slot_mask = bone_ids.T, slot_mask.T
    part, image = pl.pallas_call(
        leaf_kernel,
        out_shape=(
            jax.ShapeDtypeStruct((poses, poses), F32),
            jax.ShapeDtypeStruct((wide, poses), BF16),
        ),
        in_specs=[VMEM, SMEM, SMEM, VMEM],
        out_specs=(VMEM, VMEM),
        scratch_shapes=[pltpu.VMEM((rows // 4, poses), BF16), pltpu.VMEM((wide, poses), F32)],
        compiler_params=params(24),
        name="leaf",
    )(skin_weights, bone_ids, slot_mask, coeffs)
    gram = pl.pallas_call(
        gram_sum_kernel,
        out_shape=jax.ShapeDtypeStruct((poses, poses), F32),
        in_specs=[VMEM],
        out_specs=VMEM,
        scratch_shapes=sum_scratch(poses),
        compiler_params=params(8, collective_id=0, has_side_effects=True),
        name="gram_sum",
    )(part)
    turn, sketch = pl.pallas_call(
        turn_kernel,
        out_shape=(
            jax.ShapeDtypeStruct((RANK, poses), BF16),
            jax.ShapeDtypeStruct((RANK, wide), BF16),
        ),
        in_specs=[VMEM, VMEM],
        out_specs=(VMEM, VMEM),
        scratch_shapes=[pltpu.VMEM((1, RANK, poses), F32)],
        compiler_params=params(12),
        name="turn",
    )(gram, coeffs)
    sketches, product, joint_gram = pl.pallas_call(
        joint_kernel,
        out_shape=(
            jax.ShapeDtypeStruct((shards, RANK, wide), BF16),
            jax.ShapeDtypeStruct((joint, poses), F32),
            jax.ShapeDtypeStruct((shards // 2, shards, RANK, 2 * RANK), F32),
        ),
        in_specs=[VMEM, VMEM, VMEM],
        out_specs=(VMEM, VMEM, VMEM),
        scratch_shapes=sum_scratch(2 * RANK, (shards // 2,))
        + [
            pltpu.SemaphoreType.DMA((9,)),
            pltpu.SemaphoreType.DMA((2, shards)),
            pltpu.SemaphoreType.DMA((3, shards)),
            pltpu.SemaphoreType.DMA((3, shards)),
        ],
        compiler_params=params(20, collective_id=1, has_side_effects=True),
        name="joint",
    )(sketch, image, turn)
    basis, coefficients = pl.pallas_call(
        merge_kernel,
        out_shape=(
            jax.ShapeDtypeStruct((wide, RANK), BF16),
            jax.ShapeDtypeStruct((RANK, poses), BF16),
        ),
        in_specs=[VMEM, VMEM, VMEM],
        out_specs=(VMEM, VMEM),
        scratch_shapes=[
            pltpu.VMEM((joint, joint), F32),
            pltpu.VMEM((shards // 2, RANK, 2 * RANK), F32),
        ],
        compiler_params=params(24),
        name="merge",
    )(joint_gram, product, sketches.reshape(joint, wide))
    step_rows = rows // 2
    return pl.pallas_call(
        project_kernel,
        out_shape=jax.ShapeDtypeStruct((rows, poses), BF16),
        grid=(rows // step_rows,),
        in_specs=[
            SMEM,
            SMEM,
            pl.BlockSpec((step_rows, depth), lambda i: (i, 0)),
            VMEM,
            VMEM,
        ],
        out_specs=pl.BlockSpec((step_rows, poses), lambda i: (i, 0)),
        scratch_shapes=[pltpu.VMEM((step_rows, RANK), BF16)],
        compiler_params=params(24),
        name="project",
    )(bone_ids, slot_mask, skin_weights, basis, coefficients)


def solution(mesh):
    in_specs = (P("vtx", None), P("vtx", None), P("vtx", None), P(None, None, "pose"))
    return jax.shard_map(
        per_device, mesh=mesh, in_specs=in_specs, out_specs=P("vtx", "pose"), check_vma=False
    )
```

```python
import functools

import jax
import jax.numpy as jnp
from jax import lax
from jax.experimental import pallas as pl
from jax.experimental.pallas import tpu as pltpu
from jax.sharding import PartitionSpec as P

RANK = 64
SWEEPS = 3
SHAPES = 32
SIDE = 8
F32 = jnp.float32
BF16 = jnp.bfloat16
HIGHEST = lax.Precision.HIGHEST
MESH = pl.DeviceIdType.MESH
VMEM = pl.BlockSpec(memory_space=pltpu.VMEM)
SMEM = pl.BlockSpec(memory_space=pltpu.SMEM)


def dot(a, b, dims, precision=None):
    return lax.dot_general(a, b, (dims, ((), ())), precision=precision, preferred_element_type=F32)


NN = ((1,), (0,))
NT = ((1,), (1,))
TN = ((0,), (0,))


def chosen_rows(ids_ref, mask_ref, source_ref, block):
    parts = []
    for slot in range(ids_ref.shape[0]):
        place = pl.multiple_of(ids_ref[slot, block] * SHAPES, SHAPES)
        values = source_ref[pl.ds(place, SHAPES), :]
        parts.append(jnp.where(mask_ref[slot, block] != 0, values, jnp.zeros_like(values)))
    return jnp.concatenate(parts, axis=0)


def leaf_kernel(skin_ref, ids_ref, mask_ref, coeffs_ref, gram_ref, image_ref, slab_ref, sums_ref):
    slots, block_count = ids_ref.shape
    block_rows = skin_ref.shape[0] // block_count
    group = slab_ref.shape[0] // block_rows
    sums_ref[...] = jnp.zeros_like(sums_ref)
    gram_ref[...] = jnp.zeros_like(gram_ref)

    def step(index, carry):
        images = []
        for inside in range(group):
            block = index * group + inside
            rows = skin_ref[pl.ds(pl.multiple_of(block * block_rows, block_rows), block_rows), :]
            slab = dot(rows, chosen_rows(ids_ref, mask_ref, coeffs_ref, block), NN).astype(BF16)
            slab_ref[inside * block_rows : (inside + 1) * block_rows, :] = slab
            images.append(dot(rows, slab, TN))
        gram_ref[...] += dot(slab_ref[...], slab_ref[...], TN)
        for inside in range(group):
            block = index * group + inside
            for slot in range(slots):
                place = pl.multiple_of(ids_ref[slot, block] * SHAPES, SHAPES)
                values = images[inside][slot * SHAPES : (slot + 1) * SHAPES, :]
                sums_ref[pl.ds(place, SHAPES), :] += jnp.where(
                    mask_ref[slot, block] != 0, values, jnp.zeros_like(values)
                )
        return carry

    lax.fori_loop(0, block_count // group, step, 0)
    image_ref[...] = sums_ref[...].astype(BF16)


def my_place():
    vtx, pose = lax.axis_index("vtx"), lax.axis_index("pose")
    return vtx // SIDE, lax.rem(vtx, SIDE), pose


def vtx_peer(axis, z, y, pose, offset):
    if axis == "y":
        other = lax.rem(y + offset, SIDE)
        return other, (z * SIDE + other, pose)
    other = lax.rem(z + offset, SIDE)
    return other, (other * SIDE + y, pose)


def greet(devices, meanwhile=None):
    barrier = pltpu.get_barrier_semaphore()
    for device in devices:
        pl.semaphore_signal(barrier, inc=1, device_id=device, device_id_type=MESH)
    if meanwhile is not None:
        meanwhile()
    pl.semaphore_wait(barrier, len(devices))


def vtx_devices(z, y, pose):
    found = []
    for axis in ("y", "z"):
        for offset in range(1, SIDE):
            found.append(vtx_peer(axis, z, y, pose, offset)[1])
    return found


def exchange(parts, axis_of_half, source_of, target_of, send_sem, recv_sem, place):
    z, y, pose = place
    copies = []
    for half in range(parts):
        axis = axis_of_half[half]
        me = y if axis == "y" else z
        for offset in range(1, SIDE):
            other, device = vtx_peer(axis, z, y, pose, offset)
            copy = pltpu.make_async_remote_copy(
                src_ref=source_of(half, other),
                dst_ref=target_of(half, me),
                send_sem=send_sem.at[half, offset],
                recv_sem=recv_sem.at[half, me],
                device_id=device,
                device_id_type=MESH,
            )
            copy.start()
            copies.append(copy)
    return copies


def arrived(half, axis, target_of, send_sem, recv_sem, place):
    z, y, pose = place
    for offset in range(1, SIDE):
        other, device = vtx_peer(axis, z, y, pose, offset)
        pltpu.make_async_remote_copy(
            src_ref=target_of(half, other),
            dst_ref=target_of(half, other),
            send_sem=send_sem.at[half, offset],
            recv_sem=recv_sem.at[half, other],
            device_id=device,
            device_id_type=MESH,
        ).wait_recv()


def vtx_sum(source, first, second, total, sems, place):
    z, y, pose = place
    outer, inner = ("y", "z"), ("z", "y")
    mine = {"y": y, "z": z}
    sent = exchange(
        2, outer, lambda h, o: source.at[h, o], lambda h, m: first.at[h, m], sems[0], sems[1], place
    )
    for half in range(2):
        arrived(half, outer[half], lambda h, o: first.at[h, o], sems[0], sems[1], place)
        me = mine[outer[half]]
        first[half, me] = source[half, me]
        value = first[half, 0]
        for index in range(1, SIDE):
            value += first[half, index]
        second[half, mine[inner[half]]] = value
        sent += exchange_one(half, inner[half], second, sems[2], sems[3], place)
    for half in range(2):
        arrived(half, inner[half], lambda h, o: second.at[h, o], sems[2], sems[3], place)
        value = second[half, 0]
        for index in range(1, SIDE):
            value += second[half, index]
        total[half, mine[outer[half]]] = value
        sent += exchange_one(half, outer[half], total, sems[4], sems[5], place)
    for half in range(2):
        arrived(half, outer[half], lambda h, o: total.at[h, o], sems[4], sems[5], place)
    for copy in sent:
        copy.wait_send()


def exchange_one(half, axis, buffer, send_sem, recv_sem, place):
    z, y, pose = place
    me = y if axis == "y" else z
    copies = []
    for offset in range(1, SIDE):
        other, device = vtx_peer(axis, z, y, pose, offset)
        copy = pltpu.make_async_remote_copy(
            src_ref=buffer.at[half, me],
            dst_ref=buffer.at[half, me],
            send_sem=send_sem.at[half, offset],
            recv_sem=recv_sem.at[half, me],
            device_id=device,
            device_id_type=MESH,
        )
        copy.start()
        copies.append(copy)
    return copies


def to_chunks(matrix_ref, chunks_ref):
    depth = chunks_ref.shape[2]
    for half in range(2):
        for chunk in range(SIDE):
            chunks_ref[half, chunk] = matrix_ref[
                chunk * depth : (chunk + 1) * depth, half * 128 : (half + 1) * 128
            ]


def from_chunks(chunks_ref, matrix_ref):
    depth = chunks_ref.shape[2]
    for half in range(2):
        for chunk in range(SIDE):
            matrix_ref[chunk * depth : (chunk + 1) * depth, half * 128 : (half + 1) * 128] = chunks_ref[
                half, chunk
            ]


def gram_sum_kernel(part_ref, gram_ref, source, first, second, total, *sems):
    place = my_place()
    greet(vtx_devices(*place), lambda: to_chunks(part_ref, source))
    vtx_sum(source, first, second, total, sems, place)
    from_chunks(total, gram_ref)


def sum_scratch(rows, groups=()):
    return [pltpu.VMEM((*groups, 2, SIDE, rows // SIDE, 128), F32)] * 4 + [
        pltpu.SemaphoreType.DMA((*groups, 2, SIDE))
    ] * 6


def inverse_factors(grams):
    count = len(grams)
    groups = RANK // 8
    sublane = lax.broadcasted_iota(jnp.int32, (8, 128), 0)
    lane = lax.broadcasted_iota(jnp.int32, (8, 128), 1)
    rows = [
        [gram[8 * g : 8 * g + 8] + jnp.where(lane == sublane + 8 * g, 1.0, 0.0) for g in range(groups)]
        for gram in grams
    ]
    squares = []
    for p in range(groups):
        for n in range(count):
            own = rows[n]
            spread = [
                [
                    jnp.broadcast_to(own[g][:, RANK + 8 * p + c : RANK + 8 * p + c + 1], (8, 128))
                    for g in range(p, groups)
                ]
                for c in range(8)
            ]
            pivots = jnp.ones((8, 128), F32)
            for c in range(8):
                pivot = jnp.broadcast_to(spread[c][0][c : c + 1, :], (8, 128))
                pivots = jnp.where(sublane == c, pivot, pivots)
                inverse = 1.0 / pivot
                lead = jnp.broadcast_to(own[p][c : c + 1, :], (8, 128)) * inverse
                leads = [
                    jnp.broadcast_to(spread[d][0][c : c + 1, :], (8, 128)) * inverse
                    for d in range(c + 1, 8)
                ]
                for g in range(p, groups):
                    column = spread[c][g - p]
                    if g == p:
                        column = jnp.where(sublane > c, column, 0.0)
                    own[g] = own[g] - column * lead
                    for d in range(c + 1, 8):
                        spread[d][g - p] = spread[d][g - p] - column * leads[d - c - 1]
            own[p] = own[p] * lax.rsqrt(pivots)
            squares.append((n, pivots))
    factors = [jnp.concatenate(own, axis=0)[:, :RANK] for own in rows]
    return factors, [[value for m, value in squares if m == n] for n in range(count)]


def factors_of(columns):
    grams = []
    for value in columns:
        padded = jnp.concatenate([jnp.zeros_like(value), value], axis=0)
        grams.append(dot(value, padded, NT, HIGHEST))
    return inverse_factors(grams)


def top_spaces(grams, out_ref):
    columns = []
    scaled = []
    for gram in grams:
        size = gram.shape[0]
        diagonal = lax.broadcasted_iota(jnp.int32, (size, size), 0) == lax.broadcasted_iota(
            jnp.int32, (size, size), 1
        )
        largest = jnp.max(
            jnp.max(jnp.where(diagonal, gram, 0.0), axis=0, keepdims=True), axis=1, keepdims=True
        )
        scaled.append(gram * (1.0 / largest))
        columns.append(scaled[-1][:RANK, :])
    for sweep in range(SWEEPS - 1):
        columns = [dot(value, gram, NN, HIGHEST) for value, gram in zip(columns, scaled)]
    factors, squares = factors_of(columns)
    worst = None
    for n, (factor, value) in enumerate(zip(factors, columns)):
        out_ref[n] = dot(factor, value, NN, HIGHEST)
        low = functools.reduce(jnp.minimum, squares[n])
        high = functools.reduce(jnp.maximum, squares[n])
        ratio = jnp.min(low) / jnp.max(high)
        good = ratio > 2e-5
        worst = good if worst is None else jnp.logical_and(worst, good)

    @pl.when(jnp.logical_not(worst))
    def _():
        row = lax.broadcasted_iota(jnp.int32, grams[0].shape, 0)
        lane = lax.broadcasted_iota(jnp.int32, grams[0].shape, 1)
        for n in range(len(grams)):
            out_ref[n] = jnp.where(row == lane, 1.0, 0.0).astype(F32)[:RANK]

        def sweep(index, carry):
            values = [dot(out_ref[n], gram, NN, HIGHEST) for n, gram in enumerate(grams)]
            for n, (factor, value) in enumerate(zip(factors_of(values)[0], values)):
                out_ref[n] = dot(factor, value, NN, HIGHEST)
            return carry

        lax.fori_loop(0, SWEEPS, sweep, 0)

    return [out_ref[n] for n in range(len(grams))]


def turn_kernel(gram_ref, turn_ref, space_ref):
    turn_ref[...] = top_spaces([gram_ref[...]], space_ref)[0].astype(BF16)


def joint_kernel(coeffs_ref, image_ref, turn_ref, all_ref, product_ref, gram_ref, *scratch):
    source, first, second, total = scratch[:4]
    sems = scratch[4:10]
    send_sem, recv_sem, gram_send, gram_recv = scratch[10:]
    place = my_place()
    z, y, pose = place
    vtx = z * SIDE + y
    poses = all_ref.shape[0]
    chips = poses // 2
    width = 2 * RANK
    middle = RANK // 2
    x, core = pose // 2, lax.rem(pose, 2)
    sibling = (vtx, x * 2 + 1 - core)
    chip_at = [lax.rem(x + group, chips) for group in range(chips)]
    peer = [(vtx, chip * 2 + core) for chip in chip_at]
    outer, inner = ("y", "z"), ("z", "y")
    mine = {"y": y, "z": z}

    def own_sketch():
        all_ref[pose] = dot(turn_ref[...], coeffs_ref[...], NT).astype(BF16)

    greet(
        vtx_devices(*place) + [(vtx, lax.rem(pose + offset, poses)) for offset in range(1, poses)],
        own_sketch,
    )
    sent = []

    def send(source_ref, target_ref, arrival, device, number):
        copy = pltpu.make_async_remote_copy(
            src_ref=source_ref,
            dst_ref=target_ref,
            send_sem=send_sem.at[number],
            recv_sem=arrival,
            device_id=device,
            device_id_type=MESH,
        )
        copy.start()
        sent.append(copy)

    def wait_for(target_ref, arrival, device):
        pltpu.make_async_remote_copy(
            src_ref=target_ref,
            dst_ref=target_ref,
            send_sem=send_sem.at[0],
            recv_sem=arrival,
            device_id=device,
            device_id_type=MESH,
        ).wait_recv()

    def half_of(slot, half):
        return all_ref.at[slot, pl.ds(half * middle, middle)]

    def start_sum(group):
        pair = all_ref[pl.ds(chip_at[group] * 2, 2)].reshape(width, all_ref.shape[2])
        part = dot(pair, image_ref[...], NN)
        depth = width // SIDE
        for chunk in range(SIDE):
            for half in range(2):
                source[group, half, chunk] = part[
                    chunk * depth : (chunk + 1) * depth, half * 128 : (half + 1) * 128
                ]
        sent.extend(
            exchange(
                2,
                outer,
                lambda h, o: source.at[group, h, o],
                lambda h, m: first.at[group, h, m],
                sems[0].at[group],
                sems[1].at[group],
                place,
            )
        )

    def second_leg(group):
        for half in range(2):
            arrived(
                half, outer[half], lambda h, o: first.at[group, h, o], sems[0].at[group], sems[1].at[group], place
            )
            me = mine[outer[half]]
            first[group, half, me] = source[group, half, me]
            value = first[group, half, 0]
            for index in range(1, SIDE):
                value += first[group, half, index]
            second[group, half, mine[inner[half]]] = value
            sent.extend(
                exchange_one(half, inner[half], second.at[group], sems[2].at[group], sems[3].at[group], place)
            )

    def third_leg(group):
        for half in range(2):
            arrived(
                half, inner[half], lambda h, o: second.at[group, h, o], sems[2].at[group], sems[3].at[group], place
            )
            value = second[group, half, 0]
            for index in range(1, SIDE):
                value += second[group, half, index]
            total[group, half, mine[outer[half]]] = value
            sent.extend(
                exchange_one(half, outer[half], total.at[group], sems[4].at[group], sems[5].at[group], place)
            )

    def end_sum(group):
        for half in range(2):
            arrived(
                half, outer[half], lambda h, o: total.at[group, h, o], sems[4].at[group], sems[5].at[group], place
            )
        row = pl.multiple_of(chip_at[group] * width, width)
        for half in range(2):
            product_ref[pl.ds(row, width), half * 128 : (half + 1) * 128] = total[group, half].reshape(width, 128)

    def gram_part(group):
        row = pl.multiple_of(chip_at[group] * width, width)
        gram_ref[chip_at[group], pose] = dot(
            turn_ref[...].astype(F32), product_ref[pl.ds(row, width), :], NT, HIGHEST
        )
        for offset in range(1, poses):
            copy = pltpu.make_async_remote_copy(
                src_ref=gram_ref.at[chip_at[group], pose],
                dst_ref=gram_ref.at[chip_at[group], pose],
                send_sem=gram_send.at[group, offset],
                recv_sem=gram_recv.at[group, pose],
                device_id=(vtx, lax.rem(pose + offset, poses)),
                device_id_type=MESH,
            )
            copy.start()
            sent.append(copy)

    def gram_arrived(group):
        for offset in range(1, poses):
            other = lax.rem(pose + offset, poses)
            chip = lax.rem(other // 2 + group, chips)
            wait_for(gram_ref.at[chip, other], gram_recv.at[group, other], (vtx, other))

    up, down, across = [chip_at[g] * 2 + core for g in (1, 3, 2)]
    up_peer, down_peer = peer[1], peer[3]

    def send_half(slot, half, device, number):
        send(half_of(slot, half), half_of(slot, half), recv_sem.at[half, slot], device, number)

    def pass_on(slot, half, origin, targets, number):
        wait_for(half_of(slot, half), recv_sem.at[half, slot], origin)
        for index, device in enumerate(targets):
            send_half(slot, half, device, number + index)

    def from_sibling(group):
        slot = chip_at[group] * 2 + 1 - core
        for half in range(2):
            wait_for(half_of(slot, half), recv_sem.at[half, slot], sibling)

    send_half(pose, 0, up_peer, 0)
    send_half(pose, 1, down_peer, 1)
    for half in range(2):
        send_half(pose, half, sibling, 2 + half)
    from_sibling(0)
    start_sum(0)
    send_half(pose, 1, up_peer, 4)
    send_half(pose, 0, down_peer, 5)
    pass_on(down, 0, down_peer, (up_peer, sibling), 6)
    pass_on(up, 1, up_peer, (down_peer, sibling), 8)
    second_leg(0)
    pass_on(down, 1, down_peer, (sibling,), 10)
    pass_on(up, 0, up_peer, (sibling,), 11)
    third_leg(0)
    for group in (3, 1):
        from_sibling(group)
        start_sum(group)
    pass_on(across, 0, down_peer, (sibling,), 12)
    pass_on(across, 1, up_peer, (sibling,), 13)
    from_sibling(2)
    start_sum(2)
    end_sum(0)
    gram_part(0)
    for group in (3, 1, 2):
        second_leg(group)
    for group in (3, 1, 2):
        third_leg(group)
    end_sum(1)
    gram_part(1)
    end_sum(3)
    end_sum(2)
    gram_part(2)
    for group in (0, 1, 2):
        gram_arrived(group)
    for copy in sent:
        copy.wait_send()


def block_diagonal(blocks):
    height, width = blocks[0].shape
    rows = []
    for index, block in enumerate(blocks):
        parts = []
        if index:
            parts.append(jnp.zeros((height, width * index), F32))
        parts.append(block)
        if index + 1 < len(blocks):
            parts.append(jnp.zeros((height, width * (len(blocks) - 1 - index)), F32))
        rows.append(jnp.concatenate(parts, axis=1) if len(parts) > 1 else parts[0])
    return jnp.concatenate(rows, axis=0) if len(rows) > 1 else rows[0]


def congruence(blocks, gram):
    width = blocks[0].shape[1]
    left = jnp.concatenate(
        [
            dot(block, gram[index * width : (index + 1) * width, :], NN, HIGHEST)
            for index, block in enumerate(blocks)
        ],
        axis=0,
    )
    return jnp.concatenate(
        [
            dot(block, left[:, index * width : (index + 1) * width], NT, HIGHEST)
            for index, block in enumerate(blocks)
        ],
        axis=0,
    )


def merge_kernel(rows_ref, product_ref, all_ref, basis_ref, coefficients_ref, joint_ref, space_ref):
    width = 2 * RANK
    chips = rows_ref.shape[0]
    for chip in range(chips):
        for other in range(chips):
            behind = (chip - other) % chips == 1
            for index in range(2):
                if behind:
                    continue
                joint_ref[
                    chip * width + index * RANK : chip * width + (index + 1) * RANK,
                    other * width : (other + 1) * width,
                ] = rows_ref[other, 2 * chip + index]
    for chip in range(chips):
        other = (chip - 1) % chips
        joint_ref[chip * width : (chip + 1) * width, other * width : (other + 1) * width] = joint_ref[
            other * width : (other + 1) * width, chip * width : (chip + 1) * width
        ].T
    gram = joint_ref[...]
    merged = None
    while True:
        pairs = gram.shape[0] // width
        spaces = top_spaces(
            [gram[n * width : (n + 1) * width, n * width : (n + 1) * width] for n in range(pairs)],
            space_ref,
        )
        turn = block_diagonal(spaces)
        merged = turn if merged is None else dot(turn, merged, NN, HIGHEST)
        if pairs == 1:
            break
        gram = congruence(spaces, gram)
    merged = merged.astype(BF16)
    wide = merged.astype(F32)
    image = dot(wide, joint_ref[...], NN, HIGHEST)
    padded = jnp.concatenate([jnp.zeros_like(wide), wide], axis=0)
    factor = inverse_factors([dot(image, padded, NT, HIGHEST)])[0][0]
    moments = dot(wide, product_ref[...], NN, HIGHEST)
    half_way = dot(factor, moments, NN, HIGHEST)
    coefficients_ref[...] = dot(factor, half_way, TN, HIGHEST).astype(BF16)
    basis_ref[...] = dot(merged, all_ref[...], NN).T.astype(BF16)


def project_kernel(ids_ref, mask_ref, skin_ref, basis_ref, coefficients_ref, out_ref, rows_ref):
    block_count = ids_ref.shape[1]
    blocks_here = block_count // pl.num_programs(0)
    block_rows = out_ref.shape[0] // blocks_here
    first = pl.program_id(0) * blocks_here
    for index in range(blocks_here):
        chosen = chosen_rows(ids_ref, mask_ref, basis_ref, first + index)
        here = slice(index * block_rows, (index + 1) * block_rows)
        rows_ref[here, :] = dot(skin_ref[here, :], chosen, NN).astype(BF16)
    out_ref[...] = dot(rows_ref[...], coefficients_ref[...], NN).astype(BF16)


def params(mebibytes, **more):
    return pltpu.CompilerParams(vmem_limit_bytes=mebibytes * 2**20, **more)


def per_device(skin_weights, bone_ids, slot_mask, pose_coeffs):
    rows, depth = skin_weights.shape
    bones, shapes, poses = pose_coeffs.shape
    coeffs = pose_coeffs.reshape(bones * shapes, poses)
    wide = bones * shapes
    shards = lax.axis_size("pose")
    joint = shards * RANK
    bone_ids, slot_mask = bone_ids.T, slot_mask.T
    part, image = pl.pallas_call(
        leaf_kernel,
        out_shape=(
            jax.ShapeDtypeStruct((poses, poses), F32),
            jax.ShapeDtypeStruct((wide, poses), BF16),
        ),
        in_specs=[VMEM, SMEM, SMEM, VMEM],
        out_specs=(VMEM, VMEM),
        scratch_shapes=[pltpu.VMEM((rows // 4, poses), BF16), pltpu.VMEM((wide, poses), F32)],
        compiler_params=params(50),
        name="leaf",
    )(skin_weights, bone_ids, slot_mask, coeffs)
    gram = pl.pallas_call(
        gram_sum_kernel,
        out_shape=jax.ShapeDtypeStruct((poses, poses), F32),
        in_specs=[VMEM],
        out_specs=VMEM,
        scratch_shapes=sum_scratch(poses),
        compiler_params=params(8, collective_id=0, has_side_effects=True),
        name="gram_sum",
    )(part)
    turn = pl.pallas_call(
        turn_kernel,
        out_shape=jax.ShapeDtypeStruct((RANK, poses), BF16),
        in_specs=[VMEM],
        out_specs=VMEM,
        scratch_shapes=[pltpu.VMEM((1, RANK, poses), F32)],
        compiler_params=params(12),
        name="turn",
    )(gram)
    sketches, product, joint_gram = pl.pallas_call(
        joint_kernel,
        out_shape=(
            jax.ShapeDtypeStruct((shards, RANK, wide), BF16),
            jax.ShapeDtypeStruct((joint, poses), F32),
            jax.ShapeDtypeStruct((shards // 2, shards, RANK, 2 * RANK), F32),
        ),
        in_specs=[VMEM, VMEM, VMEM],
        out_specs=(VMEM, VMEM, VMEM),
        scratch_shapes=sum_scratch(2 * RANK, (shards // 2,))
        + [
            pltpu.SemaphoreType.DMA((14,)),
            pltpu.SemaphoreType.DMA((2, shards)),
            pltpu.SemaphoreType.DMA((3, shards)),
            pltpu.SemaphoreType.DMA((3, shards)),
        ],
        compiler_params=params(20, collective_id=1, has_side_effects=True),
        name="joint",
    )(coeffs, image, turn)
    basis, coefficients = pl.pallas_call(
        merge_kernel,
        out_shape=(
            jax.ShapeDtypeStruct((wide, RANK), BF16),
            jax.ShapeDtypeStruct((RANK, poses), BF16),
        ),
        in_specs=[VMEM, VMEM, VMEM],
        out_specs=(VMEM, VMEM),
        scratch_shapes=[
            pltpu.VMEM((joint, joint), F32),
            pltpu.VMEM((shards // 2, RANK, 2 * RANK), F32),
        ],
        compiler_params=params(24),
        name="merge",
    )(joint_gram, product, sketches.reshape(joint, wide))
    step_rows = rows // 2
    return pl.pallas_call(
        project_kernel,
        out_shape=jax.ShapeDtypeStruct((rows, poses), BF16),
        grid=(rows // step_rows,),
        in_specs=[
            SMEM,
            SMEM,
            pl.BlockSpec((step_rows, depth), lambda i: (i, 0)),
            VMEM,
            VMEM,
        ],
        out_specs=pl.BlockSpec((step_rows, poses), lambda i: (i, 0)),
        scratch_shapes=[pltpu.VMEM((step_rows, RANK), BF16)],
        compiler_params=params(24),
        name="project",
    )(bone_ids, slot_mask, skin_weights, basis, coefficients)


def solution(mesh):
    in_specs = (P("vtx", None), P("vtx", None), P("vtx", None), P(None, None, "pose"))
    return jax.shard_map(
        per_device, mesh=mesh, in_specs=in_specs, out_specs=P("vtx", "pose"), check_vma=False
    )
```

```python
import functools

import jax
import jax.numpy as jnp
from jax import lax
from jax.experimental import pallas as pl
from jax.experimental.pallas import tpu as pltpu
from jax.sharding import PartitionSpec as P

RANK = 64
SWEEPS = 3
SHAPES = 32
SIDE = 8
F32 = jnp.float32
BF16 = jnp.bfloat16
HIGHEST = lax.Precision.HIGHEST
MESH = pl.DeviceIdType.MESH
VMEM = pl.BlockSpec(memory_space=pltpu.VMEM)
SMEM = pl.BlockSpec(memory_space=pltpu.SMEM)


def dot(a, b, dims, precision=None):
    return lax.dot_general(a, b, (dims, ((), ())), precision=precision, preferred_element_type=F32)


NN = ((1,), (0,))
NT = ((1,), (1,))
TN = ((0,), (0,))


def chosen_rows(ids_ref, mask_ref, source_ref, block):
    parts = []
    for slot in range(ids_ref.shape[0]):
        place = pl.multiple_of(ids_ref[slot, block] * SHAPES, SHAPES)
        values = source_ref[pl.ds(place, SHAPES), :]
        parts.append(jnp.where(mask_ref[slot, block] != 0, values, jnp.zeros_like(values)))
    return jnp.concatenate(parts, axis=0)


def leaf_kernel(skin_ref, ids_ref, mask_ref, coeffs_ref, gram_ref, image_ref, slab_ref, sums_ref):
    slots, block_count = ids_ref.shape
    block_rows = skin_ref.shape[0] // block_count
    group = slab_ref.shape[0] // block_rows
    sums_ref[...] = jnp.zeros_like(sums_ref)
    gram_ref[...] = jnp.zeros_like(gram_ref)

    def step(index, carry):
        images = []
        for inside in range(group):
            block = index * group + inside
            rows = skin_ref[pl.ds(pl.multiple_of(block * block_rows, block_rows), block_rows), :]
            slab = dot(rows, chosen_rows(ids_ref, mask_ref, coeffs_ref, block), NN).astype(BF16)
            slab_ref[inside * block_rows : (inside + 1) * block_rows, :] = slab
            images.append(dot(rows, slab, TN))
        gram_ref[...] += dot(slab_ref[...], slab_ref[...], TN)
        for inside in range(group):
            block = index * group + inside
            for slot in range(slots):
                place = pl.multiple_of(ids_ref[slot, block] * SHAPES, SHAPES)
                values = images[inside][slot * SHAPES : (slot + 1) * SHAPES, :]
                sums_ref[pl.ds(place, SHAPES), :] += jnp.where(
                    mask_ref[slot, block] != 0, values, jnp.zeros_like(values)
                )
        return carry

    lax.fori_loop(0, block_count // group, step, 0)
    image_ref[...] = sums_ref[...].astype(BF16)


def my_place():
    vtx, pose = lax.axis_index("vtx"), lax.axis_index("pose")
    return vtx // SIDE, lax.rem(vtx, SIDE), pose


def vtx_peer(axis, z, y, pose, offset):
    if axis == "y":
        other = lax.rem(y + offset, SIDE)
        return other, (z * SIDE + other, pose)
    other = lax.rem(z + offset, SIDE)
    return other, (other * SIDE + y, pose)


def greet(devices, meanwhile=None):
    barrier = pltpu.get_barrier_semaphore()
    for device in devices:
        pl.semaphore_signal(barrier, inc=1, device_id=device, device_id_type=MESH)
    if meanwhile is not None:
        meanwhile()
    pl.semaphore_wait(barrier, len(devices))


def vtx_devices(z, y, pose):
    found = []
    for axis in ("y", "z"):
        for offset in range(1, SIDE):
            found.append(vtx_peer(axis, z, y, pose, offset)[1])
    return found


def exchange(parts, axis_of_half, source_of, target_of, send_sem, recv_sem, place):
    z, y, pose = place
    copies = []
    for half in range(parts):
        axis = axis_of_half[half]
        me = y if axis == "y" else z
        for offset in range(1, SIDE):
            other, device = vtx_peer(axis, z, y, pose, offset)
            copy = pltpu.make_async_remote_copy(
                src_ref=source_of(half, other),
                dst_ref=target_of(half, me),
                send_sem=send_sem.at[half, offset],
                recv_sem=recv_sem.at[half, me],
                device_id=device,
                device_id_type=MESH,
            )
            copy.start()
            copies.append(copy)
    return copies


def arrived(half, axis, target_of, send_sem, recv_sem, place):
    z, y, pose = place
    for offset in range(1, SIDE):
        other, device = vtx_peer(axis, z, y, pose, offset)
        pltpu.make_async_remote_copy(
            src_ref=target_of(half, other),
            dst_ref=target_of(half, other),
            send_sem=send_sem.at[half, offset],
            recv_sem=recv_sem.at[half, other],
            device_id=device,
            device_id_type=MESH,
        ).wait_recv()


def total_of(parts):
    value = parts[0].astype(F32)
    for index in range(1, SIDE):
        value += parts[index].astype(F32)
    return value


def vtx_sum(source, first, second, total, sems, place):
    z, y, pose = place
    outer, inner = ("y", "z"), ("z", "y")
    mine = {"y": y, "z": z}
    sent = exchange(
        2, outer, lambda h, o: source.at[h, o], lambda h, m: first.at[h, m], sems[0], sems[1], place
    )
    for half in range(2):
        arrived(half, outer[half], lambda h, o: first.at[h, o], sems[0], sems[1], place)
        me = mine[outer[half]]
        first[half, me] = source[half, me]
        second[half, mine[inner[half]]] = total_of(first.at[half]).astype(second.dtype)
        sent += exchange_one(half, inner[half], second, sems[2], sems[3], place)
    for half in range(2):
        arrived(half, inner[half], lambda h, o: second.at[h, o], sems[2], sems[3], place)
        total[half, mine[outer[half]]] = total_of(second.at[half]).astype(total.dtype)
        sent += exchange_one(half, outer[half], total, sems[4], sems[5], place)
    for half in range(2):
        arrived(half, outer[half], lambda h, o: total.at[h, o], sems[4], sems[5], place)
    for copy in sent:
        copy.wait_send()


def exchange_one(half, axis, buffer, send_sem, recv_sem, place):
    z, y, pose = place
    me = y if axis == "y" else z
    copies = []
    for offset in range(1, SIDE):
        other, device = vtx_peer(axis, z, y, pose, offset)
        copy = pltpu.make_async_remote_copy(
            src_ref=buffer.at[half, me],
            dst_ref=buffer.at[half, me],
            send_sem=send_sem.at[half, offset],
            recv_sem=recv_sem.at[half, me],
            device_id=device,
            device_id_type=MESH,
        )
        copy.start()
        copies.append(copy)
    return copies


def to_chunks(matrix_ref, chunks_ref):
    depth = chunks_ref.shape[2]
    for half in range(2):
        for chunk in range(SIDE):
            chunks_ref[half, chunk] = matrix_ref[
                chunk * depth : (chunk + 1) * depth, half * 128 : (half + 1) * 128
            ].astype(chunks_ref.dtype)


def from_chunks(chunks_ref, matrix_ref):
    depth = chunks_ref.shape[2]
    for half in range(2):
        for chunk in range(SIDE):
            matrix_ref[chunk * depth : (chunk + 1) * depth, half * 128 : (half + 1) * 128] = chunks_ref[
                half, chunk
            ]


def gram_sum_kernel(part_ref, gram_ref, source, first, second, total, *sems):
    place = my_place()
    greet(vtx_devices(*place), lambda: to_chunks(part_ref, source))
    vtx_sum(source, first, second, total, sems, place)
    from_chunks(total, gram_ref)


def sum_scratch(rows, last, groups=()):
    return [
        pltpu.VMEM((*groups, 2, SIDE, rows // SIDE, 128), dtype) for dtype in (BF16, BF16, BF16, last)
    ] + [pltpu.SemaphoreType.DMA((*groups, 2, SIDE))] * 6


def reciprocal(value):
    start = pl.reciprocal(value, approx=True)
    return start * (2.0 - value * start)


def inverse_factors(grams):
    count = len(grams)
    groups = RANK // 8
    sublane = lax.broadcasted_iota(jnp.int32, (8, 128), 0)
    lane = lax.broadcasted_iota(jnp.int32, (8, 128), 1)
    rows = [
        [gram[8 * g : 8 * g + 8] + jnp.where(lane == sublane + 8 * g, 1.0, 0.0) for g in range(groups)]
        for gram in grams
    ]
    squares = []
    for p in range(groups):
        for n in range(count):
            own = rows[n]
            spread = [
                [
                    jnp.broadcast_to(own[g][:, RANK + 8 * p + c : RANK + 8 * p + c + 1], (8, 128))
                    for g in range(p, groups)
                ]
                for c in range(8)
            ]
            pivots = jnp.ones((8, 128), F32)
            for c in range(8):
                pivot = jnp.broadcast_to(spread[c][0][c : c + 1, :], (8, 128))
                pivots = jnp.where(sublane == c, pivot, pivots)
                inverse = reciprocal(pivot)
                lead = jnp.broadcast_to(own[p][c : c + 1, :], (8, 128)) * inverse
                leads = [
                    jnp.broadcast_to(spread[d][0][c : c + 1, :], (8, 128)) * inverse
                    for d in range(c + 1, 8)
                ]
                for g in range(p, groups):
                    column = spread[c][g - p]
                    if g == p:
                        column = jnp.where(sublane > c, column, 0.0)
                    own[g] = own[g] - column * lead
                    for d in range(c + 1, 8):
                        spread[d][g - p] = spread[d][g - p] - column * leads[d - c - 1]
            own[p] = own[p] * lax.rsqrt(pivots)
            squares.append((n, pivots))
    factors = [jnp.concatenate(own, axis=0)[:, :RANK] for own in rows]
    return factors, [[value for m, value in squares if m == n] for n in range(count)]


def factors_of(columns):
    grams = []
    for value in columns:
        padded = jnp.concatenate([jnp.zeros_like(value), value], axis=0)
        grams.append(dot(value, padded, NT, HIGHEST))
    return inverse_factors(grams)


def scaled(gram):
    diagonal = lax.broadcasted_iota(jnp.int32, gram.shape, 0) == lax.broadcasted_iota(
        jnp.int32, gram.shape, 1
    )
    largest = jnp.max(jnp.max(jnp.where(diagonal, gram, 0.0), axis=0, keepdims=True), axis=1, keepdims=True)
    return gram * (1.0 / largest)


def top_spaces(grams, out_ref):
    columns = [gram[:RANK, :] for gram in grams]
    for sweep in range(SWEEPS - 1):
        columns = [dot(value, gram, NN, HIGHEST) for value, gram in zip(columns, grams)]
    factors, squares = factors_of(columns)
    worst = None
    for n, (factor, value) in enumerate(zip(factors, columns)):
        out_ref[n] = dot(factor, value, NN, HIGHEST)
        low = functools.reduce(jnp.minimum, squares[n])
        high = functools.reduce(jnp.maximum, squares[n])
        ratio = jnp.min(low) / jnp.max(high)
        good = ratio > 2e-5
        worst = good if worst is None else jnp.logical_and(worst, good)

    @pl.when(jnp.logical_not(worst))
    def _():
        row = lax.broadcasted_iota(jnp.int32, grams[0].shape, 0)
        lane = lax.broadcasted_iota(jnp.int32, grams[0].shape, 1)
        for n in range(len(grams)):
            out_ref[n] = jnp.where(row == lane, 1.0, 0.0).astype(F32)[:RANK]

        def sweep(index, carry):
            values = [dot(out_ref[n], gram, NN, HIGHEST) for n, gram in enumerate(grams)]
            for n, (factor, value) in enumerate(zip(factors_of(values)[0], values)):
                out_ref[n] = dot(factor, value, NN, HIGHEST)
            return carry

        lax.fori_loop(0, SWEEPS, sweep, 0)

    return [out_ref[n] for n in range(len(grams))]


def turn_kernel(gram_ref, turn_ref, space_ref):
    turn_ref[...] = top_spaces([scaled(gram_ref[...])], space_ref)[0].astype(BF16)


def joint_kernel(coeffs_ref, image_ref, turn_ref, all_ref, product_ref, own_ref, other_ref, *scratch):
    source, first, second, total = scratch[:4]
    sems = scratch[4:10]
    send_sem, recv_sem, gram_send, gram_recv = scratch[10:]
    place = my_place()
    z, y, pose = place
    vtx = z * SIDE + y
    poses = all_ref.shape[0]
    chips = poses // 2
    width = 2 * RANK
    middle = RANK // 2
    x, core = pose // 2, lax.rem(pose, 2)
    sibling = (vtx, x * 2 + 1 - core)
    chip_at = [lax.rem(x + group, chips) for group in range(chips)]
    peer = [(vtx, chip * 2 + core) for chip in chip_at]
    outer, inner = ("y", "z"), ("z", "y")
    mine = {"y": y, "z": z}

    def own_sketch():
        all_ref[pose] = dot(turn_ref[...], coeffs_ref[...], NT).astype(BF16)

    greet(
        vtx_devices(*place) + [(vtx, lax.rem(pose + offset, poses)) for offset in range(1, poses)],
        own_sketch,
    )
    sent = []

    def send(source_ref, target_ref, arrival, device, number):
        copy = pltpu.make_async_remote_copy(
            src_ref=source_ref,
            dst_ref=target_ref,
            send_sem=send_sem.at[number],
            recv_sem=arrival,
            device_id=device,
            device_id_type=MESH,
        )
        copy.start()
        sent.append(copy)

    def wait_for(target_ref, arrival, device):
        pltpu.make_async_remote_copy(
            src_ref=target_ref,
            dst_ref=target_ref,
            send_sem=send_sem.at[0],
            recv_sem=arrival,
            device_id=device,
            device_id_type=MESH,
        ).wait_recv()

    def half_of(slot, half):
        return all_ref.at[slot, pl.ds(half * middle, middle)]

    def start_sum(group):
        pair = all_ref[pl.ds(chip_at[group] * 2, 2)].reshape(width, all_ref.shape[2])
        part = dot(pair, image_ref[...], NN)
        depth = width // SIDE
        for chunk in range(SIDE):
            for half in range(2):
                source[group, half, chunk] = part[
                    chunk * depth : (chunk + 1) * depth, half * 128 : (half + 1) * 128
                ].astype(source.dtype)
        sent.extend(
            exchange(
                2,
                outer,
                lambda h, o: source.at[group, h, o],
                lambda h, m: first.at[group, h, m],
                sems[0].at[group],
                sems[1].at[group],
                place,
            )
        )

    def second_leg(group):
        for half in range(2):
            arrived(
                half, outer[half], lambda h, o: first.at[group, h, o], sems[0].at[group], sems[1].at[group], place
            )
            me = mine[outer[half]]
            first[group, half, me] = source[group, half, me]
            second[group, half, mine[inner[half]]] = total_of(first.at[group, half]).astype(second.dtype)
            sent.extend(
                exchange_one(half, inner[half], second.at[group], sems[2].at[group], sems[3].at[group], place)
            )

    def third_leg(group):
        for half in range(2):
            arrived(
                half, inner[half], lambda h, o: second.at[group, h, o], sems[2].at[group], sems[3].at[group], place
            )
            total[group, half, mine[outer[half]]] = total_of(second.at[group, half]).astype(total.dtype)
            sent.extend(
                exchange_one(half, outer[half], total.at[group], sems[4].at[group], sems[5].at[group], place)
            )

    def end_sum(group):
        for half in range(2):
            arrived(
                half, outer[half], lambda h, o: total.at[group, h, o], sems[4].at[group], sems[5].at[group], place
            )
        row = pl.multiple_of(chip_at[group] * width, width)
        for half in range(2):
            product_ref[pl.ds(row, width), half * 128 : (half + 1) * 128] = (
                total[group, half].astype(F32).reshape(width, 128)
            )

    def gram_block(group, row):
        return own_ref.at[row] if group == 0 else other_ref.at[group - 1, row]

    def gram_part(group):
        row = pl.multiple_of(chip_at[group] * width, width)
        block = gram_block(group, pose)
        block[...] = dot(turn_ref[...].astype(F32), product_ref[pl.ds(row, width), :], NT, HIGHEST).astype(
            block.dtype
        )
        for offset in range(1, poses):
            copy = pltpu.make_async_remote_copy(
                src_ref=block,
                dst_ref=block,
                send_sem=gram_send.at[group, offset],
                recv_sem=gram_recv.at[group, pose],
                device_id=(vtx, lax.rem(pose + offset, poses)),
                device_id_type=MESH,
            )
            copy.start()
            sent.append(copy)

    def gram_arrived(group):
        for offset in range(1, poses):
            other = lax.rem(pose + offset, poses)
            wait_for(gram_block(group, other), gram_recv.at[group, other], (vtx, other))

    up, down, across = [chip_at[g] * 2 + core for g in (1, 3, 2)]
    up_peer, down_peer = peer[1], peer[3]

    def send_half(slot, half, device, number):
        send(half_of(slot, half), half_of(slot, half), recv_sem.at[half, slot], device, number)

    def pass_on(slot, half, origin, targets, number):
        wait_for(half_of(slot, half), recv_sem.at[half, slot], origin)
        for index, device in enumerate(targets):
            send_half(slot, half, device, number + index)

    def from_sibling(group):
        slot = chip_at[group] * 2 + 1 - core
        for half in range(2):
            wait_for(half_of(slot, half), recv_sem.at[half, slot], sibling)

    send_half(pose, 0, up_peer, 0)
    send_half(pose, 1, down_peer, 1)
    for half in range(2):
        send_half(pose, half, sibling, 2 + half)
    from_sibling(0)
    start_sum(0)
    send_half(pose, 1, up_peer, 4)
    send_half(pose, 0, down_peer, 5)
    pass_on(down, 0, down_peer, (up_peer, sibling), 6)
    pass_on(up, 1, up_peer, (down_peer, sibling), 8)
    second_leg(0)
    pass_on(down, 1, down_peer, (sibling,), 10)
    pass_on(up, 0, up_peer, (sibling,), 11)
    third_leg(0)
    for group in (3, 1):
        from_sibling(group)
        start_sum(group)
    pass_on(across, 0, down_peer, (sibling,), 12)
    pass_on(across, 1, up_peer, (sibling,), 13)
    from_sibling(2)
    start_sum(2)
    end_sum(0)
    gram_part(0)
    for group in (3, 1, 2):
        second_leg(group)
    for group in (3, 1, 2):
        third_leg(group)
    end_sum(1)
    gram_part(1)
    end_sum(3)
    end_sum(2)
    gram_part(2)
    for group in (0, 1, 2):
        gram_arrived(group)
    for copy in sent:
        copy.wait_send()


def block_diagonal(blocks):
    height, width = blocks[0].shape
    rows = []
    for index, block in enumerate(blocks):
        parts = []
        if index:
            parts.append(jnp.zeros((height, width * index), F32))
        parts.append(block)
        if index + 1 < len(blocks):
            parts.append(jnp.zeros((height, width * (len(blocks) - 1 - index)), F32))
        rows.append(jnp.concatenate(parts, axis=1) if len(parts) > 1 else parts[0])
    return jnp.concatenate(rows, axis=0) if len(rows) > 1 else rows[0]


def congruence(blocks, gram):
    width = blocks[0].shape[1]
    left = jnp.concatenate(
        [
            dot(block, gram[index * width : (index + 1) * width, :], NN, HIGHEST)
            for index, block in enumerate(blocks)
        ],
        axis=0,
    )
    return jnp.concatenate(
        [
            dot(block, left[:, index * width : (index + 1) * width], NT, HIGHEST)
            for index, block in enumerate(blocks)
        ],
        axis=0,
    )


def merge_kernel(own_ref, other_ref, product_ref, all_ref, basis_ref, coefficients_ref, joint_ref, space_ref):
    width = 2 * RANK
    chips = own_ref.shape[0] // 2
    for chip in range(chips):
        for other in range(chips):
            group = (other - chip) % chips
            for index in range(2):
                row = 2 * chip + index
                if group < 3:
                    joint_ref[row * RANK : (row + 1) * RANK, other * width : (other + 1) * width] = (
                        own_ref[row] if group == 0 else other_ref[group - 1, row].astype(F32)
                    )
    for chip in range(chips):
        other = (chip - 1) % chips
        joint_ref[chip * width : (chip + 1) * width, other * width : (other + 1) * width] = joint_ref[
            other * width : (other + 1) * width, chip * width : (chip + 1) * width
        ].T
    gram = scaled(joint_ref[...])
    merged = None
    while True:
        pairs = gram.shape[0] // width
        spaces = top_spaces(
            [gram[n * width : (n + 1) * width, n * width : (n + 1) * width] for n in range(pairs)],
            space_ref,
        )
        turn = block_diagonal(spaces)
        merged = turn if merged is None else dot(turn, merged, NN, HIGHEST)
        if pairs == 1:
            break
        gram = congruence(spaces, gram)
    merged = merged.astype(BF16)
    wide = merged.astype(F32)
    image = dot(wide, joint_ref[...], NN, HIGHEST)
    padded = jnp.concatenate([jnp.zeros_like(wide), wide], axis=0)
    factor = inverse_factors([dot(image, padded, NT, HIGHEST)])[0][0]
    moments = dot(wide, product_ref[...], NN, HIGHEST)
    half_way = dot(factor, moments, NN, HIGHEST)
    coefficients_ref[...] = dot(factor, half_way, TN, HIGHEST).astype(BF16)
    basis_ref[...] = dot(merged, all_ref[...], NN).T.astype(BF16)


def project_kernel(ids_ref, mask_ref, skin_ref, basis_ref, coefficients_ref, out_ref, rows_ref):
    block_count = ids_ref.shape[1]
    blocks_here = block_count // pl.num_programs(0)
    block_rows = out_ref.shape[0] // blocks_here
    first = pl.program_id(0) * blocks_here
    for index in range(blocks_here):
        chosen = chosen_rows(ids_ref, mask_ref, basis_ref, first + index)
        here = slice(index * block_rows, (index + 1) * block_rows)
        rows_ref[here, :] = dot(skin_ref[here, :], chosen, NN).astype(BF16)
    out_ref[...] = dot(rows_ref[...], coefficients_ref[...], NN).astype(BF16)


def params(mebibytes, **more):
    return pltpu.CompilerParams(vmem_limit_bytes=mebibytes * 2**20, **more)


def per_device(skin_weights, bone_ids, slot_mask, pose_coeffs):
    rows, depth = skin_weights.shape
    bones, shapes, poses = pose_coeffs.shape
    coeffs = pose_coeffs.reshape(bones * shapes, poses)
    wide = bones * shapes
    shards = lax.axis_size("pose")
    joint = shards * RANK
    bone_ids, slot_mask = bone_ids.T, slot_mask.T
    part, image = pl.pallas_call(
        leaf_kernel,
        out_shape=(
            jax.ShapeDtypeStruct((poses, poses), F32),
            jax.ShapeDtypeStruct((wide, poses), BF16),
        ),
        in_specs=[VMEM, SMEM, SMEM, VMEM],
        out_specs=(VMEM, VMEM),
        scratch_shapes=[pltpu.VMEM((rows // 4, poses), BF16), pltpu.VMEM((wide, poses), F32)],
        compiler_params=params(50),
        name="leaf",
    )(skin_weights, bone_ids, slot_mask, coeffs)
    gram = pl.pallas_call(
        gram_sum_kernel,
        out_shape=jax.ShapeDtypeStruct((poses, poses), F32),
        in_specs=[VMEM],
        out_specs=VMEM,
        scratch_shapes=sum_scratch(poses, F32),
        compiler_params=params(8, collective_id=0, has_side_effects=True),
        name="gram_sum",
    )(part)
    turn = pl.pallas_call(
        turn_kernel,
        out_shape=jax.ShapeDtypeStruct((RANK, poses), BF16),
        in_specs=[VMEM],
        out_specs=VMEM,
        scratch_shapes=[pltpu.VMEM((1, RANK, poses), F32)],
        compiler_params=params(12),
        name="turn",
    )(gram)
    sketches, product, own, others = pl.pallas_call(
        joint_kernel,
        out_shape=(
            jax.ShapeDtypeStruct((shards, RANK, wide), BF16),
            jax.ShapeDtypeStruct((joint, poses), F32),
            jax.ShapeDtypeStruct((shards, RANK, 2 * RANK), F32),
            jax.ShapeDtypeStruct((2, shards, RANK, 2 * RANK), BF16),
        ),
        in_specs=[VMEM, VMEM, VMEM],
        out_specs=(VMEM, VMEM, VMEM, VMEM),
        scratch_shapes=sum_scratch(2 * RANK, BF16, (shards // 2,))
        + [
            pltpu.SemaphoreType.DMA((14,)),
            pltpu.SemaphoreType.DMA((2, shards)),
            pltpu.SemaphoreType.DMA((3, shards)),
            pltpu.SemaphoreType.DMA((3, shards)),
        ],
        compiler_params=params(20, collective_id=1, has_side_effects=True),
        name="joint",
    )(coeffs, image, turn)
    basis, coefficients = pl.pallas_call(
        merge_kernel,
        out_shape=(
            jax.ShapeDtypeStruct((wide, RANK), BF16),
            jax.ShapeDtypeStruct((RANK, poses), BF16),
        ),
        in_specs=[VMEM, VMEM, VMEM, VMEM],
        out_specs=(VMEM, VMEM),
        scratch_shapes=[
            pltpu.VMEM((joint, joint), F32),
            pltpu.VMEM((shards // 2, RANK, 2 * RANK), F32),
        ],
        compiler_params=params(24),
        name="merge",
    )(own, others, product, sketches.reshape(joint, wide))
    step_rows = rows // 2
    return pl.pallas_call(
        project_kernel,
        out_shape=jax.ShapeDtypeStruct((rows, poses), BF16),
        grid=(rows // step_rows,),
        in_specs=[
            SMEM,
            SMEM,
            pl.BlockSpec((step_rows, depth), lambda i: (i, 0)),
            VMEM,
            VMEM,
        ],
        out_specs=pl.BlockSpec((step_rows, poses), lambda i: (i, 0)),
        scratch_shapes=[pltpu.VMEM((step_rows, RANK), BF16)],
        compiler_params=params(24),
        name="project",
    )(bone_ids, slot_mask, skin_weights, basis, coefficients)


def solution(mesh):
    in_specs = (P("vtx", None), P("vtx", None), P("vtx", None), P(None, None, "pose"))
    return jax.shard_map(
        per_device, mesh=mesh, in_specs=in_specs, out_specs=P("vtx", "pose"), check_vma=False
    )
```

```python
import functools

import jax
import jax.numpy as jnp
from jax import lax
from jax.experimental import pallas as pl
from jax.experimental.pallas import tpu as pltpu
from jax.sharding import PartitionSpec as P

RANK = 64
SWEEPS = 3
SHAPES = 32
SIDE = 8
F32 = jnp.float32
BF16 = jnp.bfloat16
HIGHEST = lax.Precision.HIGHEST
MESH = pl.DeviceIdType.MESH
VMEM = pl.BlockSpec(memory_space=pltpu.VMEM)
SMEM = pl.BlockSpec(memory_space=pltpu.SMEM)


def dot(a, b, dims, precision=None):
    return lax.dot_general(a, b, (dims, ((), ())), precision=precision, preferred_element_type=F32)


NN = ((1,), (0,))
NT = ((1,), (1,))
TN = ((0,), (0,))


def chosen_rows(ids_ref, mask_ref, source_ref, block):
    parts = []
    for slot in range(ids_ref.shape[0]):
        place = pl.multiple_of(ids_ref[slot, block] * SHAPES, SHAPES)
        values = source_ref[pl.ds(place, SHAPES), :]
        parts.append(jnp.where(mask_ref[slot, block] != 0, values, jnp.zeros_like(values)))
    return jnp.concatenate(parts, axis=0)


def leaf_kernel(ids_ref, mask_ref, skin_ref, coeffs_ref, gram_ref, image_ref, slab_ref, sums_ref):
    slots, block_count = ids_ref.shape
    step, steps = pl.program_id(0), pl.num_programs(0)
    group = block_count // steps
    block_rows = skin_ref.shape[0] // group

    @pl.when(step == 0)
    def _():
        sums_ref[...] = jnp.zeros_like(sums_ref)
        gram_ref[...] = jnp.zeros_like(gram_ref)

    images = []
    for inside in range(group):
        here = slice(inside * block_rows, (inside + 1) * block_rows)
        rows = skin_ref[here, :]
        chosen = chosen_rows(ids_ref, mask_ref, coeffs_ref, step * group + inside)
        slab = dot(rows, chosen, NN).astype(BF16)
        slab_ref[here, :] = slab
        images.append(dot(rows, slab, TN))
    gram_ref[...] += dot(slab_ref[...], slab_ref[...], TN)
    for inside in range(group):
        block = step * group + inside
        for slot in range(slots):
            place = pl.multiple_of(ids_ref[slot, block] * SHAPES, SHAPES)
            values = images[inside][slot * SHAPES : (slot + 1) * SHAPES, :]
            sums_ref[pl.ds(place, SHAPES), :] += jnp.where(
                mask_ref[slot, block] != 0, values, jnp.zeros_like(values)
            )

    @pl.when(step == steps - 1)
    def _():
        image_ref[...] = sums_ref[...].astype(BF16)


def my_place():
    vtx, pose = lax.axis_index("vtx"), lax.axis_index("pose")
    return vtx // SIDE, lax.rem(vtx, SIDE), pose


def vtx_peer(axis, z, y, pose, offset):
    if axis == "y":
        other = lax.rem(y + offset, SIDE)
        return other, (z * SIDE + other, pose)
    other = lax.rem(z + offset, SIDE)
    return other, (other * SIDE + y, pose)


def greet(devices, meanwhile=None):
    barrier = pltpu.get_barrier_semaphore()
    for device in devices:
        pl.semaphore_signal(barrier, inc=1, device_id=device, device_id_type=MESH)
    if meanwhile is not None:
        meanwhile()
    pl.semaphore_wait(barrier, len(devices))


def vtx_devices(z, y, pose):
    found = []
    for axis in ("y", "z"):
        for offset in range(1, SIDE):
            found.append(vtx_peer(axis, z, y, pose, offset)[1])
    return found


def exchange(parts, axis_of_half, source_of, target_of, send_sem, recv_sem, place):
    z, y, pose = place
    copies = []
    for half in range(parts):
        axis = axis_of_half[half]
        me = y if axis == "y" else z
        for offset in range(1, SIDE):
            other, device = vtx_peer(axis, z, y, pose, offset)
            copy = pltpu.make_async_remote_copy(
                src_ref=source_of(half, other),
                dst_ref=target_of(half, me),
                send_sem=send_sem.at[half, offset],
                recv_sem=recv_sem.at[half, me],
                device_id=device,
                device_id_type=MESH,
            )
            copy.start()
            copies.append(copy)
    return copies


def arrived(half, axis, target_of, send_sem, recv_sem, place):
    z, y, pose = place
    for offset in range(1, SIDE):
        other, device = vtx_peer(axis, z, y, pose, offset)
        pltpu.make_async_remote_copy(
            src_ref=target_of(half, other),
            dst_ref=target_of(half, other),
            send_sem=send_sem.at[half, offset],
            recv_sem=recv_sem.at[half, other],
            device_id=device,
            device_id_type=MESH,
        ).wait_recv()


def total_of(parts):
    value = parts[0].astype(F32)
    for index in range(1, SIDE):
        value += parts[index].astype(F32)
    return value


def vtx_sum(source, first, second, total, sems, place):
    z, y, pose = place
    outer, inner = ("y", "z"), ("z", "y")
    mine = {"y": y, "z": z}
    sent = exchange(
        2, outer, lambda h, o: source.at[h, o], lambda h, m: first.at[h, m], sems[0], sems[1], place
    )
    for half in range(2):
        arrived(half, outer[half], lambda h, o: first.at[h, o], sems[0], sems[1], place)
        me = mine[outer[half]]
        first[half, me] = source[half, me]
        second[half, mine[inner[half]]] = total_of(first.at[half]).astype(second.dtype)
        sent += exchange_one(half, inner[half], second, sems[2], sems[3], place)
    for half in range(2):
        arrived(half, inner[half], lambda h, o: second.at[h, o], sems[2], sems[3], place)
        total[half, mine[outer[half]]] = total_of(second.at[half]).astype(total.dtype)
        sent += exchange_one(half, outer[half], total, sems[4], sems[5], place)
    for half in range(2):
        arrived(half, outer[half], lambda h, o: total.at[h, o], sems[4], sems[5], place)
    for copy in sent:
        copy.wait_send()


def exchange_one(half, axis, buffer, send_sem, recv_sem, place):
    z, y, pose = place
    me = y if axis == "y" else z
    copies = []
    for offset in range(1, SIDE):
        other, device = vtx_peer(axis, z, y, pose, offset)
        copy = pltpu.make_async_remote_copy(
            src_ref=buffer.at[half, me],
            dst_ref=buffer.at[half, me],
            send_sem=send_sem.at[half, offset],
            recv_sem=recv_sem.at[half, me],
            device_id=device,
            device_id_type=MESH,
        )
        copy.start()
        copies.append(copy)
    return copies


def to_chunks(matrix_ref, chunks_ref):
    depth = chunks_ref.shape[2]
    for half in range(2):
        for chunk in range(SIDE):
            chunks_ref[half, chunk] = matrix_ref[
                chunk * depth : (chunk + 1) * depth, half * 128 : (half + 1) * 128
            ].astype(chunks_ref.dtype)


def from_chunks(chunks_ref, matrix_ref):
    depth = chunks_ref.shape[2]
    for half in range(2):
        for chunk in range(SIDE):
            matrix_ref[chunk * depth : (chunk + 1) * depth, half * 128 : (half + 1) * 128] = chunks_ref[
                half, chunk
            ]


def gram_sum_kernel(part_ref, gram_ref, source, first, second, total, *sems):
    place = my_place()
    greet(vtx_devices(*place), lambda: to_chunks(part_ref, source))
    vtx_sum(source, first, second, total, sems, place)
    from_chunks(total, gram_ref)


def sum_scratch(rows, travels, groups=()):
    return [pltpu.VMEM((*groups, 2, SIDE, rows // SIDE, 128), travels)] * 4 + [
        pltpu.SemaphoreType.DMA((*groups, 2, SIDE))
    ] * 6


def inverse_factors(grams):
    count = len(grams)
    groups = RANK // 8
    sublane = lax.broadcasted_iota(jnp.int32, (8, 128), 0)
    lane = lax.broadcasted_iota(jnp.int32, (8, 128), 1)
    rows = [
        [gram[8 * g : 8 * g + 8] + jnp.where(lane == sublane + 8 * g, 1.0, 0.0) for g in range(groups)]
        for gram in grams
    ]
    squares = []
    for p in range(groups):
        for n in range(count):
            own = rows[n]
            spread = [
                [
                    jnp.broadcast_to(own[g][:, RANK + 8 * p + c : RANK + 8 * p + c + 1], (8, 128))
                    for g in range(p, groups)
                ]
                for c in range(8)
            ]
            pivots = jnp.ones((8, 128), F32)
            for c in range(8):
                pivot = jnp.broadcast_to(spread[c][0][c : c + 1, :], (8, 128))
                pivots = jnp.where(sublane == c, pivot, pivots)
                inverse = 1.0 / pivot
                lead = jnp.broadcast_to(own[p][c : c + 1, :], (8, 128)) * inverse
                leads = [
                    jnp.broadcast_to(spread[d][0][c : c + 1, :], (8, 128)) * inverse
                    for d in range(c + 1, 8)
                ]
                for g in range(p, groups):
                    column = spread[c][g - p]
                    if g == p:
                        column = jnp.where(sublane > c, column, 0.0)
                    own[g] = own[g] - column * lead
                    for d in range(c + 1, 8):
                        spread[d][g - p] = spread[d][g - p] - column * leads[d - c - 1]
            own[p] = own[p] * lax.rsqrt(pivots)
            squares.append((n, pivots))
    factors = [jnp.concatenate(own, axis=0)[:, :RANK] for own in rows]
    return factors, [[value for m, value in squares if m == n] for n in range(count)]


def factors_of(columns):
    grams = []
    for value in columns:
        padded = jnp.concatenate([jnp.zeros_like(value), value], axis=0)
        grams.append(dot(value, padded, NT, HIGHEST))
    return inverse_factors(grams)


def scale_of(grams):
    diagonal = lax.broadcasted_iota(jnp.int32, grams[0].shape, 0) == lax.broadcasted_iota(
        jnp.int32, grams[0].shape, 1
    )
    largest = jnp.where(diagonal, functools.reduce(jnp.maximum, grams), 0.0)
    return 1.0 / jnp.max(jnp.max(largest, axis=0, keepdims=True), axis=1, keepdims=True)


def top_spaces(grams, out_ref):
    columns = [gram[:RANK, :] for gram in grams]
    for sweep in range(SWEEPS - 1):
        columns = [dot(value, gram, NN, HIGHEST) for value, gram in zip(columns, grams)]
    factors, squares = factors_of(columns)
    worst = None
    for n, (factor, value) in enumerate(zip(factors, columns)):
        out_ref[n] = dot(factor, value, NN, HIGHEST)
        low = functools.reduce(jnp.minimum, squares[n])
        high = functools.reduce(jnp.maximum, squares[n])
        ratio = jnp.min(low) / jnp.max(high)
        good = ratio > 2e-5
        worst = good if worst is None else jnp.logical_and(worst, good)

    @pl.when(jnp.logical_not(worst))
    def _():
        row = lax.broadcasted_iota(jnp.int32, grams[0].shape, 0)
        lane = lax.broadcasted_iota(jnp.int32, grams[0].shape, 1)
        for n in range(len(grams)):
            out_ref[n] = jnp.where(row == lane, 1.0, 0.0).astype(F32)[:RANK]

        def sweep(index, carry):
            values = [dot(out_ref[n], gram, NN, HIGHEST) for n, gram in enumerate(grams)]
            for n, (factor, value) in enumerate(zip(factors_of(values)[0], values)):
                out_ref[n] = dot(factor, value, NN, HIGHEST)
            return carry

        lax.fori_loop(0, SWEEPS, sweep, 0)

    return [out_ref[n] for n in range(len(grams))]


def turn_kernel(gram_ref, turn_ref, space_ref):
    gram = gram_ref[...]
    turn_ref[...] = top_spaces([gram * scale_of([gram])], space_ref)[0].astype(BF16)


def joint_kernel(coeffs_ref, image_ref, turn_ref, all_ref, product_ref, own_ref, other_ref, *scratch):
    source, first, second, total = scratch[:4]
    sems = scratch[4:10]
    send_sem, recv_sem, gram_send, gram_recv = scratch[10:]
    place = my_place()
    z, y, pose = place
    vtx = z * SIDE + y
    poses = all_ref.shape[0]
    chips = poses // 2
    width = 2 * RANK
    middle = RANK // 2
    x, core = pose // 2, lax.rem(pose, 2)
    sibling = (vtx, x * 2 + 1 - core)
    chip_at = [lax.rem(x + group, chips) for group in range(chips)]
    peer = [(vtx, chip * 2 + core) for chip in chip_at]
    outer, inner = ("y", "z"), ("z", "y")
    mine = {"y": y, "z": z}

    def own_sketch():
        all_ref[pose] = dot(turn_ref[...], coeffs_ref[...], NT).astype(BF16)

    greet(
        vtx_devices(*place) + [(vtx, lax.rem(pose + offset, poses)) for offset in range(1, poses)],
        own_sketch,
    )
    sent = []

    def send(source_ref, target_ref, arrival, device, number):
        copy = pltpu.make_async_remote_copy(
            src_ref=source_ref,
            dst_ref=target_ref,
            send_sem=send_sem.at[number],
            recv_sem=arrival,
            device_id=device,
            device_id_type=MESH,
        )
        copy.start()
        sent.append(copy)

    def wait_for(target_ref, arrival, device):
        pltpu.make_async_remote_copy(
            src_ref=target_ref,
            dst_ref=target_ref,
            send_sem=send_sem.at[0],
            recv_sem=arrival,
            device_id=device,
            device_id_type=MESH,
        ).wait_recv()

    def half_of(slot, half):
        return all_ref.at[slot, pl.ds(half * middle, middle)]

    def start_sum(group):
        pair = all_ref[pl.ds(chip_at[group] * 2, 2)].reshape(width, all_ref.shape[2])
        part = dot(pair, image_ref[...], NN)
        depth = width // SIDE
        for chunk in range(SIDE):
            for half in range(2):
                source[group, half, chunk] = part[
                    chunk * depth : (chunk + 1) * depth, half * 128 : (half + 1) * 128
                ].astype(source.dtype)
        sent.extend(
            exchange(
                2,
                outer,
                lambda h, o: source.at[group, h, o],
                lambda h, m: first.at[group, h, m],
                sems[0].at[group],
                sems[1].at[group],
                place,
            )
        )

    def second_leg(group):
        for half in range(2):
            arrived(
                half, outer[half], lambda h, o: first.at[group, h, o], sems[0].at[group], sems[1].at[group], place
            )
            me = mine[outer[half]]
            first[group, half, me] = source[group, half, me]
            second[group, half, mine[inner[half]]] = total_of(first.at[group, half]).astype(second.dtype)
            sent.extend(
                exchange_one(half, inner[half], second.at[group], sems[2].at[group], sems[3].at[group], place)
            )

    def third_leg(group):
        for half in range(2):
            arrived(
                half, inner[half], lambda h, o: second.at[group, h, o], sems[2].at[group], sems[3].at[group], place
            )
            total[group, half, mine[outer[half]]] = total_of(second.at[group, half]).astype(total.dtype)
            sent.extend(
                exchange_one(half, outer[half], total.at[group], sems[4].at[group], sems[5].at[group], place)
            )

    def end_sum(group):
        for half in range(2):
            arrived(
                half, outer[half], lambda h, o: total.at[group, h, o], sems[4].at[group], sems[5].at[group], place
            )
        row = pl.multiple_of(chip_at[group] * width, width)
        for half in range(2):
            product_ref[pl.ds(row, width), half * 128 : (half + 1) * 128] = (
                total[group, half].astype(F32).reshape(width, 128)
            )

    def gram_block(group, row):
        return own_ref.at[row] if group == 0 else other_ref.at[group - 1, row]

    def gram_part(group):
        row = pl.multiple_of(chip_at[group] * width, width)
        block = gram_block(group, pose)
        block[...] = dot(turn_ref[...].astype(F32), product_ref[pl.ds(row, width), :], NT, HIGHEST).astype(
            block.dtype
        )
        for offset in range(1, poses):
            copy = pltpu.make_async_remote_copy(
                src_ref=block,
                dst_ref=block,
                send_sem=gram_send.at[group, offset],
                recv_sem=gram_recv.at[group, pose],
                device_id=(vtx, lax.rem(pose + offset, poses)),
                device_id_type=MESH,
            )
            copy.start()
            sent.append(copy)

    def gram_arrived(group):
        for offset in range(1, poses):
            other = lax.rem(pose + offset, poses)
            wait_for(gram_block(group, other), gram_recv.at[group, other], (vtx, other))

    up, down, across = [chip_at[g] * 2 + core for g in (1, 3, 2)]
    up_peer, down_peer = peer[1], peer[3]

    def send_half(slot, half, device, number):
        send(half_of(slot, half), half_of(slot, half), recv_sem.at[half, slot], device, number)

    def pass_on(slot, half, origin, targets, number):
        wait_for(half_of(slot, half), recv_sem.at[half, slot], origin)
        for index, device in enumerate(targets):
            send_half(slot, half, device, number + index)

    def from_sibling(group):
        slot = chip_at[group] * 2 + 1 - core
        for half in range(2):
            wait_for(half_of(slot, half), recv_sem.at[half, slot], sibling)

    send_half(pose, 0, up_peer, 0)
    send_half(pose, 1, down_peer, 1)
    for half in range(2):
        send_half(pose, half, sibling, 2 + half)
    from_sibling(0)
    start_sum(0)
    send_half(pose, 1, up_peer, 4)
    send_half(pose, 0, down_peer, 5)
    pass_on(down, 0, down_peer, (up_peer, sibling), 6)
    pass_on(up, 1, up_peer, (down_peer, sibling), 8)
    second_leg(0)
    pass_on(down, 1, down_peer, (sibling,), 10)
    pass_on(up, 0, up_peer, (sibling,), 11)
    third_leg(0)
    for group in (3, 1):
        from_sibling(group)
        start_sum(group)
    pass_on(across, 0, down_peer, (sibling,), 12)
    pass_on(across, 1, up_peer, (sibling,), 13)
    from_sibling(2)
    start_sum(2)
    end_sum(0)
    gram_part(0)
    for group in (3, 1, 2):
        second_leg(group)
    for group in (3, 1, 2):
        third_leg(group)
    end_sum(1)
    gram_part(1)
    end_sum(3)
    end_sum(2)
    gram_part(2)
    for group in (0, 1, 2):
        gram_arrived(group)
    for copy in sent:
        copy.wait_send()


def block_diagonal(blocks):
    height, width = blocks[0].shape
    rows = []
    for index, block in enumerate(blocks):
        parts = []
        if index:
            parts.append(jnp.zeros((height, width * index), F32))
        parts.append(block)
        if index + 1 < len(blocks):
            parts.append(jnp.zeros((height, width * (len(blocks) - 1 - index)), F32))
        rows.append(jnp.concatenate(parts, axis=1) if len(parts) > 1 else parts[0])
    return jnp.concatenate(rows, axis=0) if len(rows) > 1 else rows[0]


def congruence(blocks, gram):
    width = blocks[0].shape[1]
    left = jnp.concatenate(
        [
            dot(block, gram[index * width : (index + 1) * width, :], NN, HIGHEST)
            for index, block in enumerate(blocks)
        ],
        axis=0,
    )
    return jnp.concatenate(
        [
            dot(block, left[:, index * width : (index + 1) * width], NT, HIGHEST)
            for index, block in enumerate(blocks)
        ],
        axis=0,
    )


def merge_kernel(own_ref, other_ref, product_ref, all_ref, basis_ref, coefficients_ref, joint_ref, space_ref):
    width = 2 * RANK
    chips = own_ref.shape[0] // 2
    for chip in range(chips):
        for other in range(chips):
            group = (other - chip) % chips
            for index in range(2):
                row = 2 * chip + index
                if group < 3:
                    joint_ref[row * RANK : (row + 1) * RANK, other * width : (other + 1) * width] = (
                        own_ref[row] if group == 0 else other_ref[group - 1, row].astype(F32)
                    )
    for chip in range(chips):
        other = (chip - 1) % chips
        joint_ref[chip * width : (chip + 1) * width, other * width : (other + 1) * width] = joint_ref[
            other * width : (other + 1) * width, chip * width : (chip + 1) * width
        ].T
    gram = joint_ref
    blocks = [gram[n * width : (n + 1) * width, n * width : (n + 1) * width] for n in range(chips)]
    scale = scale_of(blocks)
    blocks = [block * scale for block in blocks]
    merged = None
    while True:
        spaces = top_spaces(blocks, space_ref)
        turn = block_diagonal(spaces)
        merged = turn if merged is None else dot(turn, merged, NN, HIGHEST)
        if len(spaces) == 1:
            break
        factor = scale if gram is joint_ref else 1.0
        gram = congruence(spaces, gram) * factor
        blocks = [
            gram[n * width : (n + 1) * width, n * width : (n + 1) * width] for n in range(len(spaces) // 2)
        ]
    merged = merged.astype(BF16)
    wide = merged.astype(F32)
    image = dot(wide, joint_ref[...], NN, HIGHEST)
    padded = jnp.concatenate([jnp.zeros_like(wide), wide], axis=0)
    factor = inverse_factors([dot(image, padded, NT, HIGHEST)])[0][0]
    moments = dot(wide, product_ref[...], NN, HIGHEST)
    half_way = dot(factor, moments, NN, HIGHEST)
    coefficients_ref[...] = dot(factor, half_way, TN, HIGHEST).astype(BF16)
    basis_ref[...] = dot(merged, all_ref[...], NN).T.astype(BF16)


def project_kernel(ids_ref, mask_ref, skin_ref, basis_ref, coefficients_ref, out_ref, rows_ref):
    block_count = ids_ref.shape[1]
    blocks_here = block_count // pl.num_programs(0)
    block_rows = out_ref.shape[0] // blocks_here
    first = pl.program_id(0) * blocks_here
    for index in range(blocks_here):
        chosen = chosen_rows(ids_ref, mask_ref, basis_ref, first + index)
        here = slice(index * block_rows, (index + 1) * block_rows)
        rows_ref[here, :] = dot(skin_ref[here, :], chosen, NN).astype(BF16)
    out_ref[...] = dot(rows_ref[...], coefficients_ref[...], NN).astype(BF16)


def params(mebibytes, **more):
    return pltpu.CompilerParams(vmem_limit_bytes=mebibytes * 2**20, **more)


def per_device(skin_weights, bone_ids, slot_mask, pose_coeffs):
    rows, depth = skin_weights.shape
    bones, shapes, poses = pose_coeffs.shape
    coeffs = pose_coeffs.reshape(bones * shapes, poses)
    wide = bones * shapes
    shards = lax.axis_size("pose")
    joint = shards * RANK
    bone_ids, slot_mask = bone_ids.T, slot_mask.T
    part, image = pl.pallas_call(
        leaf_kernel,
        out_shape=(
            jax.ShapeDtypeStruct((poses, poses), F32),
            jax.ShapeDtypeStruct((wide, poses), BF16),
        ),
        grid=(4,),
        in_specs=[SMEM, SMEM, pl.BlockSpec((rows // 4, depth), lambda i: (i, 0)), VMEM],
        out_specs=(VMEM, VMEM),
        scratch_shapes=[pltpu.VMEM((rows // 4, poses), BF16), pltpu.VMEM((wide, poses), F32)],
        compiler_params=params(50),
        name="leaf",
    )(bone_ids, slot_mask, skin_weights, coeffs)
    gram = pl.pallas_call(
        gram_sum_kernel,
        out_shape=jax.ShapeDtypeStruct((poses, poses), F32),
        in_specs=[VMEM],
        out_specs=VMEM,
        scratch_shapes=sum_scratch(poses, F32),
        compiler_params=params(8, collective_id=0, has_side_effects=True),
        name="gram_sum",
    )(part)
    turn = pl.pallas_call(
        turn_kernel,
        out_shape=jax.ShapeDtypeStruct((RANK, poses), BF16),
        in_specs=[VMEM],
        out_specs=VMEM,
        scratch_shapes=[pltpu.VMEM((1, RANK, poses), F32)],
        compiler_params=params(12),
        name="turn",
    )(gram)
    sketches, product, own, others = pl.pallas_call(
        joint_kernel,
        out_shape=(
            jax.ShapeDtypeStruct((shards, RANK, wide), BF16),
            jax.ShapeDtypeStruct((joint, poses), F32),
            jax.ShapeDtypeStruct((shards, RANK, 2 * RANK), F32),
            jax.ShapeDtypeStruct((2, shards, RANK, 2 * RANK), BF16),
        ),
        in_specs=[VMEM, VMEM, VMEM],
        out_specs=(VMEM, VMEM, VMEM, VMEM),
        scratch_shapes=sum_scratch(2 * RANK, BF16, (shards // 2,))
        + [
            pltpu.SemaphoreType.DMA((14,)),
            pltpu.SemaphoreType.DMA((2, shards)),
            pltpu.SemaphoreType.DMA((3, shards)),
            pltpu.SemaphoreType.DMA((3, shards)),
        ],
        compiler_params=params(20, collective_id=1, has_side_effects=True),
        name="joint",
    )(coeffs, image, turn)
    basis, coefficients = pl.pallas_call(
        merge_kernel,
        out_shape=(
            jax.ShapeDtypeStruct((wide, RANK), BF16),
            jax.ShapeDtypeStruct((RANK, poses), BF16),
        ),
        in_specs=[VMEM, VMEM, VMEM, VMEM],
        out_specs=(VMEM, VMEM),
        scratch_shapes=[
            pltpu.VMEM((joint, joint), F32),
            pltpu.VMEM((shards // 2, RANK, 2 * RANK), F32),
        ],
        compiler_params=params(24),
        name="merge",
    )(own, others, product, sketches.reshape(joint, wide))
    step_rows = rows // 2
    return pl.pallas_call(
        project_kernel,
        out_shape=jax.ShapeDtypeStruct((rows, poses), BF16),
        grid=(rows // step_rows,),
        in_specs=[
            SMEM,
            SMEM,
            pl.BlockSpec((step_rows, depth), lambda i: (i, 0)),
            VMEM,
            VMEM,
        ],
        out_specs=pl.BlockSpec((step_rows, poses), lambda i: (i, 0)),
        scratch_shapes=[pltpu.VMEM((step_rows, RANK), BF16)],
        compiler_params=params(24),
        name="project",
    )(bone_ids, slot_mask, skin_weights, basis, coefficients)


def solution(mesh):
    in_specs = (P("vtx", None), P("vtx", None), P("vtx", None), P(None, None, "pose"))
    return jax.shard_map(
        per_device, mesh=mesh, in_specs=in_specs, out_specs=P("vtx", "pose"), check_vma=False
    )
```

```python
import functools

import jax
import jax.numpy as jnp
from jax import lax
from jax.experimental import pallas as pl
from jax.experimental.pallas import tpu as pltpu
from jax.sharding import PartitionSpec as P

RANK = 64
SWEEPS = 3
SHAPES = 32
SIDE = 8
F32 = jnp.float32
BF16 = jnp.bfloat16
HIGHEST = lax.Precision.HIGHEST
MESH = pl.DeviceIdType.MESH
VMEM = pl.BlockSpec(memory_space=pltpu.VMEM)
SMEM = pl.BlockSpec(memory_space=pltpu.SMEM)


def dot(a, b, dims, precision=None):
    return lax.dot_general(a, b, (dims, ((), ())), precision=precision, preferred_element_type=F32)


NN = ((1,), (0,))
NT = ((1,), (1,))
TN = ((0,), (0,))


def chosen_rows(ids_ref, mask_ref, source_ref, block):
    parts = []
    for slot in range(ids_ref.shape[0]):
        place = pl.multiple_of(ids_ref[slot, block] * SHAPES, SHAPES)
        values = source_ref[pl.ds(place, SHAPES), :]
        parts.append(jnp.where(mask_ref[slot, block] != 0, values, jnp.zeros_like(values)))
    return jnp.concatenate(parts, axis=0)


def leaf_kernel(ids_ref, mask_ref, skin_ref, coeffs_ref, gram_ref, image_ref, slab_ref, sums_ref):
    slots, block_count = ids_ref.shape
    step, steps = pl.program_id(0), pl.num_programs(0)
    group = block_count // steps
    block_rows = skin_ref.shape[0] // group

    @pl.when(step == 0)
    def _():
        sums_ref[...] = jnp.zeros_like(sums_ref)
        gram_ref[...] = jnp.zeros_like(gram_ref)

    images = []
    for inside in range(group):
        here = slice(inside * block_rows, (inside + 1) * block_rows)
        rows = skin_ref[here, :]
        chosen = chosen_rows(ids_ref, mask_ref, coeffs_ref, step * group + inside)
        slab = dot(rows, chosen, NN).astype(BF16)
        slab_ref[here, :] = slab
        images.append(dot(rows, slab, TN))
    gram_ref[...] += dot(slab_ref[...], slab_ref[...], TN)
    for inside in range(group):
        block = step * group + inside
        for slot in range(slots):
            place = pl.multiple_of(ids_ref[slot, block] * SHAPES, SHAPES)
            values = images[inside][slot * SHAPES : (slot + 1) * SHAPES, :]
            sums_ref[pl.ds(place, SHAPES), :] += jnp.where(
                mask_ref[slot, block] != 0, values, jnp.zeros_like(values)
            )

    @pl.when(step == steps - 1)
    def _():
        image_ref[...] = sums_ref[...].astype(BF16)


def my_place():
    vtx, pose = lax.axis_index("vtx"), lax.axis_index("pose")
    return vtx // SIDE, lax.rem(vtx, SIDE), pose


def vtx_peer(axis, z, y, pose, offset):
    if axis == "y":
        other = lax.rem(y + offset, SIDE)
        return other, (z * SIDE + other, pose)
    other = lax.rem(z + offset, SIDE)
    return other, (other * SIDE + y, pose)


def greet(devices, meanwhile=None):
    barrier = pltpu.get_barrier_semaphore()
    for device in devices:
        pl.semaphore_signal(barrier, inc=1, device_id=device, device_id_type=MESH)
    if meanwhile is not None:
        meanwhile()
    pl.semaphore_wait(barrier, len(devices))


def vtx_devices(z, y, pose):
    found = []
    for axis in ("y", "z"):
        for offset in range(1, SIDE):
            found.append(vtx_peer(axis, z, y, pose, offset)[1])
    return found


def exchange(parts, axis_of_half, source_of, target_of, send_sem, recv_sem, place):
    z, y, pose = place
    copies = []
    for half in range(parts):
        axis = axis_of_half[half]
        me = y if axis == "y" else z
        for offset in range(1, SIDE):
            other, device = vtx_peer(axis, z, y, pose, offset)
            copy = pltpu.make_async_remote_copy(
                src_ref=source_of(half, other),
                dst_ref=target_of(half, me),
                send_sem=send_sem.at[half, offset],
                recv_sem=recv_sem.at[half, me],
                device_id=device,
                device_id_type=MESH,
            )
            copy.start()
            copies.append(copy)
    return copies


def arrived(half, axis, target_of, send_sem, recv_sem, place):
    z, y, pose = place
    for offset in range(1, SIDE):
        other, device = vtx_peer(axis, z, y, pose, offset)
        pltpu.make_async_remote_copy(
            src_ref=target_of(half, other),
            dst_ref=target_of(half, other),
            send_sem=send_sem.at[half, offset],
            recv_sem=recv_sem.at[half, other],
            device_id=device,
            device_id_type=MESH,
        ).wait_recv()


def total_of(parts):
    value = parts[0].astype(F32)
    for index in range(1, SIDE):
        value += parts[index].astype(F32)
    return value


def vtx_sum(source, first, second, total, sems, place):
    z, y, pose = place
    outer, inner = ("y", "z"), ("z", "y")
    mine = {"y": y, "z": z}
    sent = exchange(
        2, outer, lambda h, o: source.at[h, o], lambda h, m: first.at[h, m], sems[0], sems[1], place
    )
    for half in range(2):
        arrived(half, outer[half], lambda h, o: first.at[h, o], sems[0], sems[1], place)
        me = mine[outer[half]]
        first[half, me] = source[half, me]
        second[half, mine[inner[half]]] = total_of(first.at[half]).astype(second.dtype)
        sent += exchange_one(half, inner[half], second, sems[2], sems[3], place)
    for half in range(2):
        arrived(half, inner[half], lambda h, o: second.at[h, o], sems[2], sems[3], place)
        total[half, mine[outer[half]]] = total_of(second.at[half]).astype(total.dtype)
        sent += exchange_one(half, outer[half], total, sems[4], sems[5], place)
    for half in range(2):
        arrived(half, outer[half], lambda h, o: total.at[h, o], sems[4], sems[5], place)
    for copy in sent:
        copy.wait_send()


def exchange_one(half, axis, buffer, send_sem, recv_sem, place):
    z, y, pose = place
    me = y if axis == "y" else z
    copies = []
    for offset in range(1, SIDE):
        other, device = vtx_peer(axis, z, y, pose, offset)
        copy = pltpu.make_async_remote_copy(
            src_ref=buffer.at[half, me],
            dst_ref=buffer.at[half, me],
            send_sem=send_sem.at[half, offset],
            recv_sem=recv_sem.at[half, me],
            device_id=device,
            device_id_type=MESH,
        )
        copy.start()
        copies.append(copy)
    return copies


def to_chunks(matrix_ref, chunks_ref):
    depth = chunks_ref.shape[2]
    for half in range(2):
        for chunk in range(SIDE):
            chunks_ref[half, chunk] = matrix_ref[
                chunk * depth : (chunk + 1) * depth, half * 128 : (half + 1) * 128
            ].astype(chunks_ref.dtype)


def from_chunks(chunks_ref, matrix_ref):
    depth = chunks_ref.shape[2]
    for half in range(2):
        for chunk in range(SIDE):
            matrix_ref[chunk * depth : (chunk + 1) * depth, half * 128 : (half + 1) * 128] = chunks_ref[
                half, chunk
            ]


def gram_sum_kernel(part_ref, gram_ref, source, first, second, total, *sems):
    place = my_place()
    greet(vtx_devices(*place), lambda: to_chunks(part_ref, source))
    vtx_sum(source, first, second, total, sems, place)
    from_chunks(total, gram_ref)


def sum_scratch(rows, travels, groups=()):
    return [pltpu.VMEM((*groups, 2, SIDE, rows // SIDE, 128), travels)] * 4 + [
        pltpu.SemaphoreType.DMA((*groups, 2, SIDE))
    ] * 6


def inverse_factors(grams):
    count = len(grams)
    groups = RANK // 8
    sublane = lax.broadcasted_iota(jnp.int32, (8, 128), 0)
    lane = lax.broadcasted_iota(jnp.int32, (8, 128), 1)
    rows = [
        [gram[8 * g : 8 * g + 8] + jnp.where(lane == sublane + 8 * g, 1.0, 0.0) for g in range(groups)]
        for gram in grams
    ]
    squares = []
    for p in range(groups):
        for n in range(count):
            own = rows[n]
            spread = [
                [
                    jnp.broadcast_to(own[g][:, RANK + 8 * p + c : RANK + 8 * p + c + 1], (8, 128))
                    for g in range(p, groups)
                ]
                for c in range(8)
            ]
            pivots = jnp.ones((8, 128), F32)
            for c in range(8):
                pivot = jnp.broadcast_to(spread[c][0][c : c + 1, :], (8, 128))
                pivots = jnp.where(sublane == c, pivot, pivots)
                inverse = 1.0 / pivot
                lead = jnp.broadcast_to(own[p][c : c + 1, :], (8, 128)) * inverse
                leads = [
                    jnp.broadcast_to(spread[d][0][c : c + 1, :], (8, 128)) * inverse
                    for d in range(c + 1, 8)
                ]
                for g in range(p, groups):
                    column = spread[c][g - p]
                    if g == p:
                        column = jnp.where(sublane > c, column, 0.0)
                    own[g] = own[g] - column * lead
                    for d in range(c + 1, 8):
                        spread[d][g - p] = spread[d][g - p] - column * leads[d - c - 1]
            own[p] = own[p] * lax.rsqrt(pivots)
            squares.append((n, pivots))
    factors = [jnp.concatenate(own, axis=0)[:, :RANK] for own in rows]
    return factors, [[value for m, value in squares if m == n] for n in range(count)]


def factors_of(columns):
    grams = []
    for value in columns:
        padded = jnp.concatenate([jnp.zeros_like(value), value], axis=0)
        grams.append(dot(value, padded, NT, HIGHEST))
    return inverse_factors(grams)


def scale_of(grams):
    diagonal = lax.broadcasted_iota(jnp.int32, grams[0].shape, 0) == lax.broadcasted_iota(
        jnp.int32, grams[0].shape, 1
    )
    largest = jnp.where(diagonal, functools.reduce(jnp.maximum, grams), 0.0)
    return 1.0 / jnp.max(jnp.max(largest, axis=0, keepdims=True), axis=1, keepdims=True)


def top_spaces(grams, out_ref):
    columns = [gram[:RANK, :] for gram in grams]
    for sweep in range(SWEEPS - 1):
        columns = [dot(value, gram, NN, HIGHEST) for value, gram in zip(columns, grams)]
    factors, squares = factors_of(columns)
    worst = None
    for n, (factor, value) in enumerate(zip(factors, columns)):
        out_ref[n] = dot(factor, value, NN, HIGHEST)
        low = functools.reduce(jnp.minimum, squares[n])
        high = functools.reduce(jnp.maximum, squares[n])
        ratio = jnp.min(low) / jnp.max(high)
        good = ratio > 2e-5
        worst = good if worst is None else jnp.logical_and(worst, good)

    @pl.when(jnp.logical_not(worst))
    def _():
        row = lax.broadcasted_iota(jnp.int32, grams[0].shape, 0)
        lane = lax.broadcasted_iota(jnp.int32, grams[0].shape, 1)
        for n in range(len(grams)):
            out_ref[n] = jnp.where(row == lane, 1.0, 0.0).astype(F32)[:RANK]

        def sweep(index, carry):
            values = [dot(out_ref[n], gram, NN, HIGHEST) for n, gram in enumerate(grams)]
            for n, (factor, value) in enumerate(zip(factors_of(values)[0], values)):
                out_ref[n] = dot(factor, value, NN, HIGHEST)
            return carry

        lax.fori_loop(0, SWEEPS, sweep, 0)

    return [out_ref[n] for n in range(len(grams))]


def turn_kernel(gram_ref, turn_ref, space_ref):
    gram = gram_ref[...]
    turn_ref[...] = top_spaces([gram * scale_of([gram])], space_ref)[0].astype(BF16)


def joint_kernel(coeffs_ref, image_ref, turn_ref, all_ref, product_ref, own_ref, other_ref, *scratch):
    source, first, second, total = scratch[:4]
    sems = scratch[4:10]
    send_sem, recv_sem, gram_send, gram_recv = scratch[10:]
    place = my_place()
    z, y, pose = place
    vtx = z * SIDE + y
    poses = all_ref.shape[0]
    chips = poses // 2
    width = 2 * RANK
    middle = RANK // 2
    x, core = pose // 2, lax.rem(pose, 2)
    sibling = (vtx, x * 2 + 1 - core)
    chip_at = [lax.rem(x + group, chips) for group in range(chips)]
    peer = [(vtx, chip * 2 + core) for chip in chip_at]
    outer, inner = ("y", "z"), ("z", "y")
    mine = {"y": y, "z": z}

    def own_sketch():
        all_ref[pose] = dot(turn_ref[...], coeffs_ref[...], NT).astype(BF16)

    greet(
        vtx_devices(*place) + [(vtx, lax.rem(pose + offset, poses)) for offset in range(1, poses)],
        own_sketch,
    )
    sent = []

    def send(source_ref, target_ref, arrival, device, number):
        copy = pltpu.make_async_remote_copy(
            src_ref=source_ref,
            dst_ref=target_ref,
            send_sem=send_sem.at[number],
            recv_sem=arrival,
            device_id=device,
            device_id_type=MESH,
        )
        copy.start()
        sent.append(copy)

    def wait_for(target_ref, arrival, device):
        pltpu.make_async_remote_copy(
            src_ref=target_ref,
            dst_ref=target_ref,
            send_sem=send_sem.at[0],
            recv_sem=arrival,
            device_id=device,
            device_id_type=MESH,
        ).wait_recv()

    def half_of(slot, half):
        return all_ref.at[slot, pl.ds(half * middle, middle)]

    def start_sum(group):
        pair = all_ref[pl.ds(chip_at[group] * 2, 2)].reshape(width, all_ref.shape[2])
        part = dot(pair, image_ref[...], NN)
        depth = width // SIDE
        for chunk in range(SIDE):
            for half in range(2):
                source[group, half, chunk] = part[
                    chunk * depth : (chunk + 1) * depth, half * 128 : (half + 1) * 128
                ].astype(source.dtype)
        sent.extend(
            exchange(
                2,
                outer,
                lambda h, o: source.at[group, h, o],
                lambda h, m: first.at[group, h, m],
                sems[0].at[group],
                sems[1].at[group],
                place,
            )
        )

    def second_leg(group):
        for half in range(2):
            arrived(
                half, outer[half], lambda h, o: first.at[group, h, o], sems[0].at[group], sems[1].at[group], place
            )
            me = mine[outer[half]]
            first[group, half, me] = source[group, half, me]
            second[group, half, mine[inner[half]]] = total_of(first.at[group, half]).astype(second.dtype)
            sent.extend(
                exchange_one(half, inner[half], second.at[group], sems[2].at[group], sems[3].at[group], place)
            )

    def third_leg(group):
        for half in range(2):
            arrived(
                half, inner[half], lambda h, o: second.at[group, h, o], sems[2].at[group], sems[3].at[group], place
            )
            total[group, half, mine[outer[half]]] = total_of(second.at[group, half]).astype(total.dtype)
            sent.extend(
                exchange_one(half, outer[half], total.at[group], sems[4].at[group], sems[5].at[group], place)
            )

    def end_sum(group):
        for half in range(2):
            arrived(
                half, outer[half], lambda h, o: total.at[group, h, o], sems[4].at[group], sems[5].at[group], place
            )
        row = pl.multiple_of(chip_at[group] * width, width)
        for half in range(2):
            product_ref[pl.ds(row, width), half * 128 : (half + 1) * 128] = (
                total[group, half].astype(F32).reshape(width, 128)
            )

    def gram_block(group, row):
        return own_ref.at[row] if group == 0 else other_ref.at[group - 1, row]

    def gram_part(group):
        row = pl.multiple_of(chip_at[group] * width, width)
        block = gram_block(group, pose)
        block[...] = dot(turn_ref[...].astype(F32), product_ref[pl.ds(row, width), :], NT, HIGHEST).astype(
            block.dtype
        )
        for offset in range(1, poses):
            copy = pltpu.make_async_remote_copy(
                src_ref=block,
                dst_ref=block,
                send_sem=gram_send.at[group, offset],
                recv_sem=gram_recv.at[group, pose],
                device_id=(vtx, lax.rem(pose + offset, poses)),
                device_id_type=MESH,
            )
            copy.start()
            sent.append(copy)

    def gram_arrived(group):
        for offset in range(1, poses):
            other = lax.rem(pose + offset, poses)
            wait_for(gram_block(group, other), gram_recv.at[group, other], (vtx, other))

    up, down, across = [chip_at[g] * 2 + core for g in (1, 3, 2)]
    up_peer, down_peer = peer[1], peer[3]

    def send_half(slot, half, device, number):
        send(half_of(slot, half), half_of(slot, half), recv_sem.at[half, slot], device, number)

    def pass_on(slot, half, origin, targets, number):
        wait_for(half_of(slot, half), recv_sem.at[half, slot], origin)
        for index, device in enumerate(targets):
            send_half(slot, half, device, number + index)

    def from_sibling(group):
        slot = chip_at[group] * 2 + 1 - core
        for half in range(2):
            wait_for(half_of(slot, half), recv_sem.at[half, slot], sibling)

    send_half(pose, 0, up_peer, 0)
    send_half(pose, 1, down_peer, 1)
    for half in range(2):
        send_half(pose, half, sibling, 2 + half)
    from_sibling(0)
    start_sum(0)
    send_half(pose, 1, up_peer, 4)
    send_half(pose, 0, down_peer, 5)
    pass_on(down, 0, down_peer, (up_peer, sibling), 6)
    pass_on(up, 1, up_peer, (down_peer, sibling), 8)
    second_leg(0)
    pass_on(down, 1, down_peer, (sibling,), 10)
    pass_on(up, 0, up_peer, (sibling,), 11)
    third_leg(0)
    for group in (3, 1):
        from_sibling(group)
        start_sum(group)
    pass_on(across, 0, down_peer, (sibling,), 12)
    pass_on(across, 1, up_peer, (sibling,), 13)
    from_sibling(2)
    start_sum(2)
    end_sum(0)
    gram_part(0)
    for group in (3, 1, 2):
        second_leg(group)
    for group in (3, 1, 2):
        third_leg(group)
    end_sum(1)
    gram_part(1)
    end_sum(3)
    end_sum(2)
    gram_part(2)
    for group in (0, 1, 2):
        gram_arrived(group)
    for copy in sent:
        copy.wait_send()


def block_diagonal(blocks):
    height, width = blocks[0].shape
    rows = []
    for index, block in enumerate(blocks):
        parts = []
        if index:
            parts.append(jnp.zeros((height, width * index), F32))
        parts.append(block)
        if index + 1 < len(blocks):
            parts.append(jnp.zeros((height, width * (len(blocks) - 1 - index)), F32))
        rows.append(jnp.concatenate(parts, axis=1) if len(parts) > 1 else parts[0])
    return jnp.concatenate(rows, axis=0) if len(rows) > 1 else rows[0]


def congruence(blocks, gram):
    width = blocks[0].shape[1]
    left = jnp.concatenate(
        [
            dot(block, gram[index * width : (index + 1) * width, :], NN, HIGHEST)
            for index, block in enumerate(blocks)
        ],
        axis=0,
    )
    return jnp.concatenate(
        [
            dot(block, left[:, index * width : (index + 1) * width], NT, HIGHEST)
            for index, block in enumerate(blocks)
        ],
        axis=0,
    )


def merge_kernel(own_ref, other_ref, product_ref, all_ref, basis_ref, coefficients_ref, joint_ref, space_ref):
    width = 2 * RANK
    chips = own_ref.shape[0] // 2
    for chip in range(chips):
        for other in range(chips):
            group = (other - chip) % chips
            for index in range(2):
                row = 2 * chip + index
                if group < 3:
                    joint_ref[row * RANK : (row + 1) * RANK, other * width : (other + 1) * width] = (
                        own_ref[row] if group == 0 else other_ref[group - 1, row].astype(F32)
                    )
    for chip in range(chips):
        other = (chip - 1) % chips
        joint_ref[chip * width : (chip + 1) * width, other * width : (other + 1) * width] = joint_ref[
            other * width : (other + 1) * width, chip * width : (chip + 1) * width
        ].T
    gram = joint_ref
    blocks = [gram[n * width : (n + 1) * width, n * width : (n + 1) * width] for n in range(chips)]
    scale = scale_of(blocks)
    blocks = [block * scale for block in blocks]
    merged = None
    while True:
        spaces = top_spaces(blocks, space_ref)
        turn = block_diagonal(spaces)
        merged = turn if merged is None else dot(turn, merged, NN, HIGHEST)
        if len(spaces) == 1:
            break
        factor = scale if gram is joint_ref else 1.0
        gram = congruence(spaces, gram) * factor
        blocks = [
            gram[n * width : (n + 1) * width, n * width : (n + 1) * width] for n in range(len(spaces) // 2)
        ]
    merged = merged.astype(BF16)
    wide = merged.astype(F32)
    image = dot(wide, joint_ref[...], NN, HIGHEST)
    padded = jnp.concatenate([jnp.zeros_like(wide), wide], axis=0)
    factor = inverse_factors([dot(image, padded, NT, HIGHEST)])[0][0]
    moments = dot(wide, product_ref[...], NN, HIGHEST)
    half_way = dot(factor, moments, NN, HIGHEST)
    coefficients_ref[...] = dot(factor, half_way, TN, HIGHEST).astype(BF16)
    basis_ref[...] = dot(merged, all_ref[...], NN).T.astype(BF16)


def project_kernel(ids_ref, mask_ref, skin_ref, basis_ref, coefficients_ref, out_ref, rows_ref):
    block_count = ids_ref.shape[1]
    blocks_here = block_count // pl.num_programs(0)
    block_rows = out_ref.shape[0] // blocks_here
    first = pl.program_id(0) * blocks_here
    for index in range(blocks_here):
        chosen = chosen_rows(ids_ref, mask_ref, basis_ref, first + index)
        here = slice(index * block_rows, (index + 1) * block_rows)
        rows_ref[here, :] = dot(skin_ref[here, :], chosen, NN).astype(BF16)
    out_ref[...] = dot(rows_ref[...], coefficients_ref[...], NN).astype(BF16)


def params(mebibytes, **more):
    return pltpu.CompilerParams(vmem_limit_bytes=mebibytes * 2**20, **more)


def per_device(skin_weights, bone_ids, slot_mask, pose_coeffs):
    rows, depth = skin_weights.shape
    bones, shapes, poses = pose_coeffs.shape
    coeffs = pose_coeffs.reshape(bones * shapes, poses)
    wide = bones * shapes
    shards = lax.axis_size("pose")
    joint = shards * RANK
    bone_ids, slot_mask = bone_ids.T, slot_mask.T
    part, image = pl.pallas_call(
        leaf_kernel,
        out_shape=(
            jax.ShapeDtypeStruct((poses, poses), F32),
            jax.ShapeDtypeStruct((wide, poses), BF16),
        ),
        grid=(2,),
        in_specs=[SMEM, SMEM, pl.BlockSpec((rows // 2, depth), lambda i: (i, 0)), VMEM],
        out_specs=(VMEM, VMEM),
        scratch_shapes=[pltpu.VMEM((rows // 2, poses), BF16), pltpu.VMEM((wide, poses), F32)],
        compiler_params=params(50),
        name="leaf",
    )(bone_ids, slot_mask, skin_weights, coeffs)
    gram = pl.pallas_call(
        gram_sum_kernel,
        out_shape=jax.ShapeDtypeStruct((poses, poses), F32),
        in_specs=[VMEM],
        out_specs=VMEM,
        scratch_shapes=sum_scratch(poses, F32),
        compiler_params=params(8, collective_id=0, has_side_effects=True),
        name="gram_sum",
    )(part)
    turn = pl.pallas_call(
        turn_kernel,
        out_shape=jax.ShapeDtypeStruct((RANK, poses), BF16),
        in_specs=[VMEM],
        out_specs=VMEM,
        scratch_shapes=[pltpu.VMEM((1, RANK, poses), F32)],
        compiler_params=params(12),
        name="turn",
    )(gram)
    sketches, product, own, others = pl.pallas_call(
        joint_kernel,
        out_shape=(
            jax.ShapeDtypeStruct((shards, RANK, wide), BF16),
            jax.ShapeDtypeStruct((joint, poses), F32),
            jax.ShapeDtypeStruct((shards, RANK, 2 * RANK), F32),
            jax.ShapeDtypeStruct((2, shards, RANK, 2 * RANK), BF16),
        ),
        in_specs=[VMEM, VMEM, VMEM],
        out_specs=(VMEM, VMEM, VMEM, VMEM),
        scratch_shapes=sum_scratch(2 * RANK, BF16, (shards // 2,))
        + [
            pltpu.SemaphoreType.DMA((14,)),
            pltpu.SemaphoreType.DMA((2, shards)),
            pltpu.SemaphoreType.DMA((3, shards)),
            pltpu.SemaphoreType.DMA((3, shards)),
        ],
        compiler_params=params(20, collective_id=1, has_side_effects=True),
        name="joint",
    )(coeffs, image, turn)
    basis, coefficients = pl.pallas_call(
        merge_kernel,
        out_shape=(
            jax.ShapeDtypeStruct((wide, RANK), BF16),
            jax.ShapeDtypeStruct((RANK, poses), BF16),
        ),
        in_specs=[VMEM, VMEM, VMEM, VMEM],
        out_specs=(VMEM, VMEM),
        scratch_shapes=[
            pltpu.VMEM((joint, joint), F32),
            pltpu.VMEM((shards // 2, RANK, 2 * RANK), F32),
        ],
        compiler_params=params(24),
        name="merge",
    )(own, others, product, sketches.reshape(joint, wide))
    step_rows = rows // 2
    return pl.pallas_call(
        project_kernel,
        out_shape=jax.ShapeDtypeStruct((rows, poses), BF16),
        grid=(rows // step_rows,),
        in_specs=[
            SMEM,
            SMEM,
            pl.BlockSpec((step_rows, depth), lambda i: (i, 0)),
            VMEM,
            VMEM,
        ],
        out_specs=pl.BlockSpec((step_rows, poses), lambda i: (i, 0)),
        scratch_shapes=[pltpu.VMEM((step_rows, RANK), BF16)],
        compiler_params=params(24),
        name="project",
    )(bone_ids, slot_mask, skin_weights, basis, coefficients)


def solution(mesh):
    in_specs = (P("vtx", None), P("vtx", None), P("vtx", None), P(None, None, "pose"))
    return jax.shard_map(
        per_device, mesh=mesh, in_specs=in_specs, out_specs=P("vtx", "pose"), check_vma=False
    )
```
